32 devices in a mesh: aux: 8 (over z, y), rep: 4 (over x, core).
Axes of the slice: x: 2, y: 2, z: 4, core: 2. Of those that a mesh axis runs over, the one named last changes fastest.
Arguments:
- b_slab: bfloat16 [6144, 16, 2048], P('aux', None, 'rep'), may hold values from -0.19921875 to 0.19921875
- energy_occ: float32 [16], replicated, may hold values from -1.6 to -0.4
- energy_vir: float32 [2048], replicated, may hold values from 0.3 to 3
- owner: int32 [16], replicated, may hold values from 0 to 15, each once
- tasks: int32 [8, 2, 3], P('aux'), may hold values from 0 to 15, as said below
- counts: int32 [8], P('aux'), may hold values from 1 to 2, as said below
Outputs:
- virtual_density: float32 [2048, 2048], P('rep', 'aux')
- occupied_density: float32 [16], replicated
The draws below stay inside these ranges and needn't reach their ends.
Inputs may be any that keep to these rules, and one draw needn't show every extreme that they name: tasks[k, t, 0] and tasks[k, t, 1] lie in 0 to 1, tasks[k, t, 2] in 0 to 15. `counts`: some index has all 2 slots live.
All inputs are finite; a program needn't handle non-finite values.
Results may differ from the reference program's by a relative error of at most 0.0045.
Values may be sent and summed in bfloat16 or wider, within the bound.
A program may use at most 128 MiB of HBM per device.

```python
import jax
import jax.numpy as jnp
from jax import lax

NAUX = 6144
NV = 2048
BLK = 128
OCC_DEV = 2
TASKS = 2
NO = 16
N_AUX = 8


def draw_tasks(key, part):
    key = jax.random.fold_in(key, 11)
    first_key, second_key, third_key = jax.random.split(key, 3)
    slots = jax.random.randint(first_key, (N_AUX, TASKS, 2), 0, OCC_DEV)
    blocks = jax.random.randint(second_key, (N_AUX, TASKS, 1), 0, NV // BLK)
    chosen = jax.random.randint(third_key, (2,), 0, N_AUX * TASKS)
    flat_blocks = blocks.reshape(-1).at[chosen[0]].set(NV // BLK - 1)
    flat_slots = slots.reshape(N_AUX * TASKS, 2).at[chosen[1], 0].set(0)
    merged = jnp.concatenate([flat_slots, flat_blocks[:, None]], axis=1)
    return merged.reshape(N_AUX, TASKS, 3).astype(jnp.int32)


def draw_counts(key, part):
    key = jax.random.fold_in(key, 23)
    first_key, second_key = jax.random.split(key)
    values = jax.random.randint(first_key, (N_AUX,), 1, TASKS + 1)
    chosen = jax.random.randint(second_key, (), 0, N_AUX)
    values = values.at[(chosen + 1) % N_AUX].set(1)
    values = values.at[chosen].set(TASKS)
    return values.astype(jnp.int32)


def steps_of(rng, dims, cuts, smallest, top_value):
    gain = 1.0
    for dim, shards_of in cuts:
        steps = jax.random.uniform(jax.random.fold_in(jax.random.fold_in(rng, 6), dim), (shards_of,), jnp.float32, smallest / len(cuts), top_value / len(cuts))
        gain = gain * jnp.repeat(jnp.exp(steps), dims[dim] // shards_of).reshape((-1,) + (1,) * (len(dims) - 1 - dim))
    return gain


def noise(own_key, dims, scale, most, pieces=(), held_as=jnp.bfloat16):
    drawn = scale * jax.random.normal(own_key, dims, jnp.float32)
    if pieces:
        drawn = drawn * steps_of(own_key, dims, pieces, -0.22, 0.18)
    return jnp.clip(drawn, -most, most).astype(held_as)


def setup_inputs(seed: int = 0) -> dict:
    splits = jax.random.split(jax.random.key(seed), 7)
    b_slab = noise(splits[0], (NAUX, NO, NV), 0.036, 0.19921875, ((0, 8), (2, 4)))
    energy_occ = jnp.clip(jax.random.uniform(splits[1], (NO,), jnp.float32, -1.6, -0.4), -1.6, -0.4)
    energy_vir = jnp.clip(jax.random.uniform(splits[2], (NV,), jnp.float32, 0.3, 3.0), 0.3, 3.0)
    owner = jax.random.permutation(splits[3], NO).astype(jnp.int32)
    tasks = draw_tasks(jax.random.fold_in(splits[6], 71), 0)
    counts = draw_counts(jax.random.fold_in(splits[6], 71), 0)
    return dict(b_slab=b_slab, energy_occ=energy_occ, energy_vir=energy_vir, owner=owner, tasks=tasks, counts=counts)


def reference(b_slab, energy_occ, energy_vir, owner, tasks, counts):
    def one_task(carry, index):
        virtual_sum, occupied_sum = carry
        aux_rank = index // TASKS
        task_slot = index % TASKS
        task_row = tasks[aux_rank, task_slot]
        first_orb = owner[aux_rank * OCC_DEV + task_row[0]].astype(jnp.int32)
        second_orb = owner[aux_rank * OCC_DEV + task_row[1]].astype(jnp.int32)
        start = (task_row[2] * BLK).astype(jnp.int32)
        zero_index = jnp.zeros((), jnp.int32)
        left_cols = lax.dynamic_index_in_dim(b_slab, first_orb, 1, keepdims=False)
        right_cols = lax.dynamic_slice(b_slab, (zero_index, second_orb, start), (NAUX, 1, BLK))[:, 0, :]
        coulomb = lax.dot_general(right_cols, left_cols, (((0,), (0,)), ((), ())), preferred_element_type=jnp.float32)
        block_energy = lax.dynamic_slice_in_dim(energy_vir, start, BLK)
        denominator = energy_occ[first_orb] + energy_occ[second_orb] - block_energy[:, None] - energy_vir[None, :]
        amplitude = jnp.where(task_slot < counts[aux_rank], coulomb / denominator, jnp.zeros_like(coulomb))
        pair_weight = jnp.sum(amplitude * amplitude)
        occupied_sum = occupied_sum.at[first_orb].add(-pair_weight).at[second_orb].add(-pair_weight)
        amp_half = amplitude.astype(jnp.bfloat16)
        virtual_sum = virtual_sum + lax.dot_general(amp_half, amp_half, (((0,), (0,)), ((), ())), preferred_element_type=jnp.float32)
        return (virtual_sum, occupied_sum), None

    start_carry = (jnp.zeros((NV, NV), jnp.float32), jnp.zeros((NO,), jnp.float32))
    (virtual_sum, occupied_sum), _ = lax.scan(one_task, start_carry, jnp.arange(N_AUX * TASKS, dtype=jnp.int32))
    return virtual_sum, occupied_sum
```

```python
import jax
import jax.numpy as jnp
from jax import lax
from jax.sharding import PartitionSpec as P

BLK = 128


def local(b_slab, energy_occ, energy_vir, owner, tasks, counts):
    aux_count = lax.axis_size("aux")
    rep_count = lax.axis_size("rep")
    width = b_slab.shape[2]
    slots = tasks.shape[1]
    occ_total = owner.shape[0]
    occ_local = occ_total // aux_count
    total = energy_vir.shape[0]
    rep_rank = lax.axis_index("rep")
    aux_rank = lax.axis_index("aux")
    rows = jnp.concatenate([tasks.reshape(1, -1), counts.reshape(1, 1)], axis=1)
    rows = lax.all_gather(rows, "aux", axis=0, tiled=True)
    all_tasks = rows[:, :-1].reshape(aux_count, slots, 3)
    base = jnp.arange(aux_count, dtype=jnp.int32)[:, None] * occ_local
    first = owner[base + all_tasks[:, :, 0]].reshape(-1)
    second = owner[base + all_tasks[:, :, 1]].reshape(-1)
    start = all_tasks[:, :, 2].reshape(-1) * BLK
    holder = start // width
    within = start - holder * width
    number = first.shape[0]

    blocks = []
    for t in range(number):
        piece = lax.dynamic_slice(b_slab, (0, second[t], within[t]), (b_slab.shape[0], 1, BLK))[:, 0, :]
        blocks.append(jnp.where(holder[t] == rep_rank, piece, jnp.zeros_like(piece)))
    right = lax.psum(jnp.stack(blocks), "rep")
    left = jnp.take(b_slab, first, axis=1)
    part = jnp.einsum("tpc,pta->tca", right, left, preferred_element_type=jnp.float32)
    coulomb = lax.psum_scatter(part, "aux", scatter_dimension=0, tiled=True)

    mine = lambda v: lax.dynamic_slice_in_dim(v, aux_rank * slots, slots)
    my_first, my_second, my_start = mine(first), mine(second), mine(start)
    quarter = lax.dynamic_slice_in_dim(energy_vir, rep_rank * width, width)
    pair = energy_occ[my_first] + energy_occ[my_second]
    block_energy = jnp.stack([lax.dynamic_slice_in_dim(energy_vir, my_start[t], BLK) for t in range(slots)])
    denominator = pair[:, None, None] - block_energy[:, :, None] - quarter[None, None, :]
    live = jnp.arange(slots, dtype=jnp.int32) < counts[0]
    amplitude = jnp.where(live[:, None, None], coulomb / denominator, jnp.zeros_like(coulomb))
    weight = jnp.sum(amplitude * amplitude, axis=(1, 2))
    orbs = jnp.arange(occ_total, dtype=jnp.int32)
    hits = (my_first[:, None] == orbs).astype(jnp.float32) + (my_second[:, None] == orbs).astype(jnp.float32)
    occupied = lax.psum(-jnp.sum(weight[:, None] * hits, axis=0), ("aux", "rep"))

    amp = amplitude.astype(jnp.bfloat16).reshape(slots * BLK, width)
    amps = lax.all_gather(amp, "aux", axis=0, tiled=True)
    cols = total // aux_count
    where = aux_rank * cols
    own = lax.dynamic_slice_in_dim(amps, lax.rem(where, width), cols, 1)
    own = jnp.where(where // width == rep_rank, own, jnp.zeros_like(own))
    own = lax.psum(own, "rep")
    density = lax.dot_general(amps, own, (((0,), (0,)), ((), ())), preferred_element_type=jnp.float32)
    return density, occupied


def solution(mesh):
    return jax.shard_map(
        local,
        mesh=mesh,
        in_specs=(P("aux", None, "rep"), P(), P(), P(), P("aux", None, None), P("aux")),
        out_specs=(P("rep", "aux"), P()),
        check_vma=False,
    )
```

```python
import jax
import jax.numpy as jnp
from jax import lax
from jax.experimental import pallas as pl
from jax.experimental.pallas import tpu as pltpu
from jax.sharding import PartitionSpec as P

BLK = 128


def plain(b_slab, energy_occ, energy_vir, owner, tasks, counts):
    aux_count = lax.axis_size("aux")
    rep_count = lax.axis_size("rep")
    width = b_slab.shape[2]
    slots = tasks.shape[1]
    occ_total = owner.shape[0]
    occ_local = occ_total // aux_count
    total = energy_vir.shape[0]
    rep_rank = lax.axis_index("rep")
    aux_rank = lax.axis_index("aux")
    rows = jnp.concatenate([tasks.reshape(1, -1), counts.reshape(1, 1)], axis=1)
    rows = lax.all_gather(rows, "aux", axis=0, tiled=True)
    all_tasks = rows[:, :-1].reshape(aux_count, slots, 3)
    base = jnp.arange(aux_count, dtype=jnp.int32)[:, None] * occ_local
    first = owner[base + all_tasks[:, :, 0]].reshape(-1)
    second = owner[base + all_tasks[:, :, 1]].reshape(-1)
    start = all_tasks[:, :, 2].reshape(-1) * BLK
    holder = start // width
    within = start - holder * width
    number = first.shape[0]

    blocks = []
    for t in range(number):
        piece = lax.dynamic_slice(b_slab, (0, second[t], within[t]), (b_slab.shape[0], 1, BLK))[:, 0, :]
        blocks.append(jnp.where(holder[t] == rep_rank, piece, jnp.zeros_like(piece)))
    right = lax.psum(jnp.stack(blocks), "rep")
    left = jnp.take(b_slab, first, axis=1)
    part = jnp.einsum("tpc,pta->tca", right, left, preferred_element_type=jnp.float32)
    coulomb = lax.psum_scatter(part, "aux", scatter_dimension=0, tiled=True)

    mine = lambda v: lax.dynamic_slice_in_dim(v, aux_rank * slots, slots)
    my_first, my_second, my_start = mine(first), mine(second), mine(start)
    quarter = lax.dynamic_slice_in_dim(energy_vir, rep_rank * width, width)
    pair = energy_occ[my_first] + energy_occ[my_second]
    block_energy = jnp.stack([lax.dynamic_slice_in_dim(energy_vir, my_start[t], BLK) for t in range(slots)])
    denominator = pair[:, None, None] - block_energy[:, :, None] - quarter[None, None, :]
    live = jnp.arange(slots, dtype=jnp.int32) < counts[0]
    amplitude = jnp.where(live[:, None, None], coulomb / denominator, jnp.zeros_like(coulomb))
    weight = jnp.sum(amplitude * amplitude, axis=(1, 2))
    orbs = jnp.arange(occ_total, dtype=jnp.int32)
    hits = (my_first[:, None] == orbs).astype(jnp.float32) + (my_second[:, None] == orbs).astype(jnp.float32)
    occupied = lax.psum(-jnp.sum(weight[:, None] * hits, axis=0), ("aux", "rep"))

    amp = amplitude.astype(jnp.bfloat16).reshape(slots * BLK, width)
    amps = lax.all_gather(amp, "aux", axis=0, tiled=True)
    cols = total // aux_count
    where = aux_rank * cols
    own = lax.dynamic_slice_in_dim(amps, lax.rem(where, width), cols, 1)
    own = jnp.where(where // width == rep_rank, own, jnp.zeros_like(own))
    own = lax.psum(own, "rep")
    density = lax.dot_general(amps, own, (((0,), (0,)), ((), ())), preferred_element_type=jnp.float32)
    return density, occupied


MESH = pl.DeviceIdType.MESH


def greet(peers):
    barrier = pltpu.get_barrier_semaphore()
    for peer in peers:
        pl.semaphore_signal(barrier, inc=1, device_id=peer, device_id_type=MESH)
    pl.semaphore_wait(barrier, len(peers))


def send(src, dst, send_sem, recv_sem, peer):
    return pltpu.make_async_remote_copy(
        src_ref=src, dst_ref=dst, send_sem=send_sem, recv_sem=recv_sem, device_id=peer, device_id_type=MESH
    )


def spread_rows(row_ref, rows_ref, mine, landed, rows_send, rows_recv):
    p = lax.axis_index("aux")
    r = lax.axis_index("rep")
    peers = [(lax.rem(p + 1 + s, 8), r) for s in range(7)]
    greet(peers)
    mine[...] = row_ref[...]
    landed[p] = row_ref[...]
    copies = [send(mine, landed.at[p], rows_send.at[s], rows_recv.at[s], peers[s]) for s in range(7)]
    for copy in copies:
        copy.start()
    for copy in copies:
        copy.wait()
    rows_ref[...] = landed[...]


def select(rows, owner, e_occ, b_ref, e_row, e_col, left, cut, coef, hits, wide):
    p = lax.axis_index("aux")
    r = lax.axis_index("rep")
    depth, orbs, width = b_ref.shape

    def orbital(k, s, which):
        return owner[2 * k + rows[k, 0, 3 * s + which]]

    for g in range(width // BLK):
        wide[g] = b_ref[:, :, g * BLK:(g + 1) * BLK].astype(jnp.float32).reshape(depth * orbs, BLK)
    for k in range(8):
        for s in range(2):
            i, j = orbital(k, s, 0), orbital(k, s, 1)
            for g in range(width // BLK):
                left[2 * k + s, :, g * BLK:(g + 1) * BLK] = wide[g, pl.ds(i, depth, stride=orbs), :].astype(jnp.bfloat16)
            start = rows[k, 0, 3 * s + 2] * BLK
            holder = start // width
            within = (start - holder * width) // BLK
            mask = jnp.where(holder == r, 1.0, 0.0)
            cut[k, s] = (wide[within, pl.ds(j, depth, stride=orbs), :] * mask).astype(jnp.bfloat16)

    @pl.when(pl.program_id(0) == 0)
    def _():
        lanes = lax.broadcasted_iota(jnp.int32, (8, BLK), 1)
        quarter = e_row[:, pl.ds(pl.multiple_of(r * width, BLK), width)]
        for s in range(2):
            i, j = orbital(p, s, 0), orbital(p, s, 1)
            start = pl.multiple_of(rows[p, 0, 3 * s + 2] * BLK, BLK)
            live = jnp.where(s < rows[p, 0, 6], 1.0, 0.0)
            denominator = (e_occ[i] + e_occ[j]) - e_col[pl.ds(start, BLK), :] - quarter
            coef[s * BLK:(s + 1) * BLK, :] = live / denominator
            hits[s] = (lanes == i).astype(jnp.float32) + (lanes == j).astype(jnp.float32)


def pairs(cut, left, coef, hits, dens, occ,
          cut_in, chip, chip_in, block, y_out, y_in, acc, up_in, down_in, amps, own, occ_rep, occ_aux, occ_sum,
          a_s, a_r, b_s, b_r, c_s, c_r, y_s, y_r, z_s, u_r, d_r, gu_s, gd_s, gy_s, g_r, h_s, h_r, or_s, or_r, oa_s, oa_r):
    p = lax.axis_index("aux")
    r = lax.axis_index("rep")
    z, y = p // 2, lax.rem(p, 2)
    core = lax.rem(r, 2)
    twin = (p, r + 1 - 2 * core)
    across = (p, lax.rem(r + 2, 4))
    y_peer = (p + 1 - 2 * y, r)
    above = (lax.rem(p + 2, 8), r)
    below = (lax.rem(p + 6, 8), r)
    reps = [(p, lax.rem(r + 1 + s, 4)) for s in range(3)]
    auxes = [(lax.rem(p + 1 + s, 8), r) for s in range(7)]
    width = left.shape[2]
    cols = own.shape[2]
    greet(reps + auxes)

    def place(m):
        first = jnp.where(m == 0, 3, jnp.where(m == 1, 0, jnp.where(m == 2, 2, 1)))
        return first + (z // 2) * (3 - 2 * first)

    def copy_a(k):
        return send(cut.at[k, 1 - core], cut_in.at[k], a_s.at[k], a_r.at[k], twin)

    def copy_b(k):
        return send(chip.at[k], chip_in.at[k], b_s.at[k], b_r.at[k], across)

    def copy_c(k, half):
        return send(block.at[k, half], block.at[k, half], c_s.at[k], c_r.at[k], twin)

    def phase_a(m, carry):
        for u in range(2):
            k = 2 * place(m) + u
            copy_a(k).start()
        return carry

    def phase_b(m, carry):
        for u in range(2):
            k = 2 * place(m) + u
            copy_a(k).wait_recv()
            chip[k] = cut[k, core] + cut_in[k]
            copy_b(k).start()
        return carry

    lax.fori_loop(0, 4, phase_a, 0)
    lax.fori_loop(0, 4, phase_b, 0)

    def copy_y(t):
        return send(y_out.at[t], y_in.at[t], y_s.at[t], y_r.at[t], y_peer)

    def copy_up(t):
        return send(acc.at[t], up_in.at[t], z_s.at[t], u_r.at[t], above)

    def copy_down(t):
        return send(acc.at[t], down_in.at[t], z_s.at[t], d_r.at[t], below)

    def gather_sum(t):
        copy_y(t).wait_recv()
        acc[t] = acc[t] + y_in[t]

        @pl.when((z <= t) & (z > 0))
        def _():
            copy_up(t).wait_recv()
            acc[t] = acc[t] + up_in[t]

        @pl.when((z >= t) & (z < 3))
        def _():
            copy_down(t).wait_recv()
            acc[t] = acc[t] + down_in[t]

    def pass_on(t):
        @pl.when(t != z)
        def _():
            gather_sum(t)

        @pl.when(t > z)
        def _():
            copy_up(t).start()

        @pl.when(t < z)
        def _():
            copy_down(t).start()

    def phase_c(m, carry):
        t = place(m)
        for u in range(2):
            k = 2 * t + u
            copy_b(k).wait_recv()
            block[k, core] = chip[k] + chip_in[k]
            copy_c(k, core).start()
        for u in range(2):
            k = 2 * t + (1 - y if u == 0 else y)
            copy_c(k, 1 - core).wait_recv()
            for s in range(2):
                part = lax.dot_general(
                    block[k, s], left[2 * k + s], (((0,), (0,)), ((), ())),
                    preferred_element_type=jnp.float32,
                )
                if u == 0:
                    y_out[t, s * BLK:(s + 1) * BLK, :] = part
                else:
                    acc[t, s * BLK:(s + 1) * BLK, :] = part
            if u == 0:
                copy_y(t).start()

        @pl.when(m > 0)
        def _():
            pass_on(place(m - 1))

        return carry

    lax.fori_loop(0, 4, phase_c, 0)
    pass_on(place(3))
    gather_sum(z)

    found = jnp.zeros((8, BLK), jnp.float32)
    for s in range(2):
        amplitude = acc[z, s * BLK:(s + 1) * BLK, :] * coef[s * BLK:(s + 1) * BLK, :]
        square = jnp.sum(amplitude * amplitude, axis=0, keepdims=True)
        weight = jnp.sum(square, axis=1, keepdims=True)
        found = found - weight * hits[s]
        amps[p, s * BLK:(s + 1) * BLK, :] = amplitude.astype(jnp.bfloat16)
    occ_rep[r] = found

    def copy_or(s):
        return send(occ_rep.at[r], occ_rep.at[r], or_s.at[s], or_r.at[s], reps[s])

    def copy_oa(s):
        return send(occ_sum, occ_aux.at[p], oa_s.at[s], oa_r.at[s], auxes[s])

    holder = (p * cols) // width
    offset = pl.multiple_of(p * cols - holder * width, BLK)

    def copy_gu(k):
        return send(amps.at[k], amps.at[k], gu_s.at[k], g_r.at[k], above)

    def copy_gd(k):
        return send(amps.at[k], amps.at[k], gd_s.at[k], g_r.at[k], below)

    def copy_gy(k):
        return send(amps.at[k], amps.at[k], gy_s.at[k], g_r.at[k], y_peer)

    def copy_h(k, s):
        return send(amps.at[k, :, pl.ds(offset, cols)], own.at[k], h_s.at[k, s], h_r.at[k], reps[s])

    def share(k):
        @pl.when(r == holder)
        def _():
            for s in range(3):
                copy_h(k, s).start()
            own[k] = amps[k, :, pl.ds(offset, cols)]

    def when_up(k, d, act):
        @pl.when((z < 3) & (d <= 0))
        def _():
            act(copy_gu(k))

    def when_down(k, d, act):
        @pl.when((z > 0) & (d >= 0))
        def _():
            act(copy_gd(k))

    def each(act_fn):
        for d in (0, 1, -1, 2, -2, 3, -3):
            t = z + d

            @pl.when((t >= 0) & (t < 4))
            def _():
                act_fn(t, d)

    def gather(t, d):
        k = 2 * t + y
        if d != 0:
            copy_gy(k).wait_recv()
        when_up(k, d, lambda c: c.start())
        when_down(k, d, lambda c: c.start())
        copy_gy(k).start()
        share(k)

    def gather_y(t, d):
        k = 2 * t + 1 - y
        copy_gy(k).wait_recv()
        share(k)

    def both(t, d):
        gather(t, d)
        if d == 0:
            for s in range(3):
                copy_or(s).start()

    each(both)
    for s in range(3):
        copy_or(s).wait_recv()
    occ_sum[...] = occ_rep[0] + occ_rep[1] + occ_rep[2] + occ_rep[3]
    occ_aux[p] = occ_sum[...]
    for s in range(7):
        copy_oa(s).start()
    each(gather_y)

    @pl.when(r != holder)
    def _():
        for k in range(8):
            copy_h(k, 0).wait_recv()

    dens[...] = lax.dot_general(
        amps[...].reshape(8 * 2 * BLK, width), own[...].reshape(8 * 2 * BLK, cols),
        (((0,), (0,)), ((), ())), preferred_element_type=jnp.float32,
    )
    for s in range(7):
        copy_oa(s).wait_recv()
    total = occ_aux[0]
    for k in range(1, 8):
        total = total + occ_aux[k]
    occ[...] = total

    for k in range(8):
        copy_a(k).wait_send()
        copy_b(k).wait_send()
        copy_c(k, core).wait_send()
    for t in range(4):
        copy_y(t).wait_send()

        @pl.when(t != z)
        def _():
            copy_up(t).wait_send()

    def sent(t, d):
        k = 2 * t + y
        when_up(k, d, lambda c: c.wait_send())
        when_down(k, d, lambda c: c.wait_send())
        copy_gy(k).wait_send()

    each(sent)

    @pl.when(r == holder)
    def _():
        for k in range(8):
            for s in range(3):
                copy_h(k, s).wait_send()

    for s in range(3):
        copy_or(s).wait_send()
    for s in range(7):
        copy_oa(s).wait_send()


def local(b_slab, energy_occ, energy_vir, owner, tasks, counts):
    depth, orbs, width = b_slab.shape
    total = energy_vir.shape[0]
    row = jnp.concatenate([tasks.reshape(-1), counts.reshape(-1)])
    row = jnp.broadcast_to(jnp.pad(row, (0, BLK - row.shape[0]))[None], (8, BLK))
    part = 96
    dma = pltpu.SemaphoreType.DMA
    vmem = pl.BlockSpec(memory_space=pltpu.VMEM)
    f32, bf16 = jnp.float32, jnp.bfloat16
    rows = pl.pallas_call(
        spread_rows,
        out_shape=jax.ShapeDtypeStruct((8, 8, BLK), jnp.int32),
        in_specs=[vmem],
        out_specs=vmem,
        scratch_shapes=[
            pltpu.VMEM((8, BLK), jnp.int32), pltpu.VMEM((8, 8, BLK), jnp.int32), dma((7,)), dma((7,)),
        ],
        compiler_params=pltpu.CompilerParams(collective_id=0, has_side_effects=True),
    )(row)
    left, cut, coef, hits = pl.pallas_call(
        select,
        grid_spec=pltpu.PrefetchScalarGridSpec(
            num_scalar_prefetch=3,
            grid=(depth // part,),
            in_specs=[
                pl.BlockSpec((part, orbs, width), lambda i, *_: (i, 0, 0)),
                pl.BlockSpec((1, total), lambda i, *_: (0, 0)),
                pl.BlockSpec((total, 1), lambda i, *_: (0, 0)),
            ],
            out_specs=(
                pl.BlockSpec((16, part, width), lambda i, *_: (0, i, 0)),
                pl.BlockSpec((8, 2, part, BLK), lambda i, *_: (0, 0, i, 0)),
                pl.BlockSpec((2 * BLK, width), lambda i, *_: (0, 0)),
                pl.BlockSpec((2, 8, BLK), lambda i, *_: (0, 0, 0)),
            ),
            scratch_shapes=[pltpu.VMEM((width // BLK, part * orbs, BLK), f32)],
        ),
        out_shape=(
            jax.ShapeDtypeStruct((16, depth, width), bf16),
            jax.ShapeDtypeStruct((8, 2, depth, BLK), bf16),
            jax.ShapeDtypeStruct((2 * BLK, width), f32),
            jax.ShapeDtypeStruct((2, 8, BLK), f32),
        ),
        compiler_params=pltpu.CompilerParams(vmem_limit_bytes=32 * 2**20),
    )(rows, owner, energy_occ, b_slab, energy_vir.reshape(1, -1), energy_vir.reshape(-1, 1))
    cols = total // 8
    density, occupied = pl.pallas_call(
        pairs,
        out_shape=(
            jax.ShapeDtypeStruct((width, cols), f32),
            jax.ShapeDtypeStruct((8, BLK), f32),
        ),
        in_specs=[vmem, vmem, vmem, vmem],
        out_specs=(vmem, vmem),
        scratch_shapes=[
            pltpu.VMEM((8, depth, BLK), bf16),
            pltpu.VMEM((8, depth, BLK), bf16),
            pltpu.VMEM((8, depth, BLK), bf16),
            pltpu.VMEM((8, 2, depth, BLK), bf16),
            pltpu.VMEM((4, 2 * BLK, width), f32),
            pltpu.VMEM((4, 2 * BLK, width), f32),
            pltpu.VMEM((4, 2 * BLK, width), f32),
            pltpu.VMEM((4, 2 * BLK, width), f32),
            pltpu.VMEM((4, 2 * BLK, width), f32),
            pltpu.VMEM((8, 2 * BLK, width), bf16),
            pltpu.VMEM((8, 2 * BLK, cols), bf16),
            pltpu.VMEM((4, 8, BLK), f32),
            pltpu.VMEM((8, 8, BLK), f32),
            pltpu.VMEM((8, BLK), f32),
            dma((8,)), dma((8,)), dma((8,)), dma((8,)), dma((8,)), dma((8,)),
            dma((4,)), dma((4,)), dma((4,)), dma((4,)), dma((4,)),
            dma((8,)), dma((8,)), dma((8,)), dma((8,)),
            dma((8, 3)), dma((8,)),
            dma((3,)), dma((3,)), dma((7,)), dma((7,)),
        ],
        compiler_params=pltpu.CompilerParams(
            collective_id=1, has_side_effects=True, vmem_limit_bytes=56 * 2**20
        ),
    )(cut, left, coef, hits)
    return density, occupied[0, : owner.shape[0]]


def solution(mesh):
    fits = mesh.shape["aux"] == 8 and mesh.shape["rep"] == 4
    return jax.shard_map(
        local if fits else plain,
        mesh=mesh,
        in_specs=(P("aux", None, "rep"), P(), P(), P(), P("aux", None, None), P("aux")),
        out_specs=(P("rep", "aux"), P()),
        check_vma=False,
    )
```

```python
import functools

import jax
import jax.numpy as jnp
from jax import lax
from jax.experimental import pallas as pl
from jax.experimental.pallas import tpu as pltpu
from jax.sharding import PartitionSpec as P

BLK = 128


def plain(b_slab, energy_occ, energy_vir, owner, tasks, counts):
    aux_count = lax.axis_size("aux")
    rep_count = lax.axis_size("rep")
    width = b_slab.shape[2]
    slots = tasks.shape[1]
    occ_total = owner.shape[0]
    occ_local = occ_total // aux_count
    total = energy_vir.shape[0]
    rep_rank = lax.axis_index("rep")
    aux_rank = lax.axis_index("aux")
    rows = jnp.concatenate([tasks.reshape(1, -1), counts.reshape(1, 1)], axis=1)
    rows = lax.all_gather(rows, "aux", axis=0, tiled=True)
    all_tasks = rows[:, :-1].reshape(aux_count, slots, 3)
    base = jnp.arange(aux_count, dtype=jnp.int32)[:, None] * occ_local
    first = owner[base + all_tasks[:, :, 0]].reshape(-1)
    second = owner[base + all_tasks[:, :, 1]].reshape(-1)
    start = all_tasks[:, :, 2].reshape(-1) * BLK
    holder = start // width
    within = start - holder * width
    number = first.shape[0]

    blocks = []
    for t in range(number):
        piece = lax.dynamic_slice(b_slab, (0, second[t], within[t]), (b_slab.shape[0], 1, BLK))[:, 0, :]
        blocks.append(jnp.where(holder[t] == rep_rank, piece, jnp.zeros_like(piece)))
    right = lax.psum(jnp.stack(blocks), "rep")
    left = jnp.take(b_slab, first, axis=1)
    part = jnp.einsum("tpc,pta->tca", right, left, preferred_element_type=jnp.float32)
    coulomb = lax.psum_scatter(part, "aux", scatter_dimension=0, tiled=True)

    mine = lambda v: lax.dynamic_slice_in_dim(v, aux_rank * slots, slots)
    my_first, my_second, my_start = mine(first), mine(second), mine(start)
    quarter = lax.dynamic_slice_in_dim(energy_vir, rep_rank * width, width)
    pair = energy_occ[my_first] + energy_occ[my_second]
    block_energy = jnp.stack([lax.dynamic_slice_in_dim(energy_vir, my_start[t], BLK) for t in range(slots)])
    denominator = pair[:, None, None] - block_energy[:, :, None] - quarter[None, None, :]
    live = jnp.arange(slots, dtype=jnp.int32) < counts[0]
    amplitude = jnp.where(live[:, None, None], coulomb / denominator, jnp.zeros_like(coulomb))
    weight = jnp.sum(amplitude * amplitude, axis=(1, 2))
    orbs = jnp.arange(occ_total, dtype=jnp.int32)
    hits = (my_first[:, None] == orbs).astype(jnp.float32) + (my_second[:, None] == orbs).astype(jnp.float32)
    occupied = lax.psum(-jnp.sum(weight[:, None] * hits, axis=0), ("aux", "rep"))

    amp = amplitude.astype(jnp.bfloat16).reshape(slots * BLK, width)
    amps = lax.all_gather(amp, "aux", axis=0, tiled=True)
    cols = total // aux_count
    where = aux_rank * cols
    own = lax.dynamic_slice_in_dim(amps, lax.rem(where, width), cols, 1)
    own = jnp.where(where // width == rep_rank, own, jnp.zeros_like(own))
    own = lax.psum(own, "rep")
    density = lax.dot_general(amps, own, (((0,), (0,)), ((), ())), preferred_element_type=jnp.float32)
    return density, occupied


MESH = pl.DeviceIdType.MESH


def greet(peers):
    barrier = pltpu.get_barrier_semaphore()
    for peer in peers:
        pl.semaphore_signal(barrier, inc=1, device_id=peer, device_id_type=MESH)
    pl.semaphore_wait(barrier, len(peers))


def send(src, dst, send_sem, recv_sem, peer):
    return pltpu.make_async_remote_copy(
        src_ref=src, dst_ref=dst, send_sem=send_sem, recv_sem=recv_sem, device_id=peer, device_id_type=MESH
    )


def spread_rows(row_ref, rows_ref, mine, landed, rows_send, rows_recv):
    p = lax.axis_index("aux")
    r = lax.axis_index("rep")
    peers = [(lax.rem(p + 1 + s, 8), r) for s in range(7)]
    greet(peers)
    mine[...] = row_ref[...]
    landed[p] = row_ref[...]
    copies = [send(mine, landed.at[p], rows_send.at[s], rows_recv.at[s], peers[s]) for s in range(7)]
    for copy in copies:
        copy.start()
    for copy in copies:
        copy.wait()
    rows_ref[...] = landed[...]


def select(rows, order, valid, owner, e_occ, b_ref, e_row, e_col, left, cut, coef, hits, wide):
    p = lax.axis_index("aux")
    r = lax.axis_index("rep")
    depth, orbs, width = b_ref.shape

    def field(k, s, which):
        task = order[2 * k + s]
        return rows[task // 2, 0, 3 * lax.rem(task, 2) + which]

    def orbital(k, s, which):
        return owner[order[2 * k + s] // 2 * 2 + field(k, s, which)]

    for g in range(width // BLK):
        wide[g] = b_ref[:, :, g * BLK:(g + 1) * BLK].astype(jnp.float32).reshape(depth * orbs, BLK)
    for k in range(8):
        for s in range(2):
            i, j = orbital(k, s, 0), orbital(k, s, 1)
            for g in range(width // BLK):
                left[2 * k + s, :, g * BLK:(g + 1) * BLK] = wide[g, pl.ds(i, depth, stride=orbs), :].astype(jnp.bfloat16)
            start = field(k, s, 2) * BLK
            holder = start // width
            within = (start - holder * width) // BLK
            mask = jnp.where(holder == r, 1.0, 0.0)
            cut[k, s] = (wide[within, pl.ds(j, depth, stride=orbs), :] * mask).astype(jnp.bfloat16)

    @pl.when(pl.program_id(0) == 0)
    def _():
        lanes = lax.broadcasted_iota(jnp.int32, (8, BLK), 1)
        quarter = e_row[:, pl.ds(pl.multiple_of(r * width, BLK), width)]
        for s in range(2):
            i, j = orbital(p, s, 0), orbital(p, s, 1)
            start = pl.multiple_of(field(p, s, 2) * BLK, BLK)
            live = jnp.where(valid[2 * p + s] > 0, 1.0, 0.0)
            denominator = (e_occ[i] + e_occ[j]) - e_col[pl.ds(start, BLK), :] - quarter
            coef[s * BLK:(s + 1) * BLK, :] = live / denominator
            hits[s] = (lanes == i).astype(jnp.float32) + (lanes == j).astype(jnp.float32)


def pack(dst, x):
    rows = x.shape[0]
    top = jnp.max(jnp.abs(x), axis=0, keepdims=True)
    power = jnp.ceil(jnp.log2(jnp.maximum(top, 1e-30)))
    scaled = jnp.floor(x * jnp.exp2(14.0 - power) + 0.5)
    dst[:rows, :] = scaled.astype(jnp.int32).astype(jnp.int16)
    dst[rows:, :] = jnp.broadcast_to(power, (16, x.shape[1])).astype(jnp.int32).astype(jnp.int16)


def unpack(src):
    rows = src.shape[0] - 16
    power = src[rows:, :].astype(jnp.int32).astype(jnp.float32)[:1]
    return src[:rows, :].astype(jnp.int32).astype(jnp.float32) * jnp.exp2(power - 14.0)


def pairs(one_way, cut, left_hbm, coef, hits, dens, occ,
          left, left_sem, part_out, z_out, e_s, e_r, cut_in, chip, chip_in, block, y_out, y_in, acc, up_in, down_in, amps, own, occ_rep, occ_aux, occ_sum,
          a_s, a_r, b_s, b_r, c_s, c_r, y_s, y_r, z_s, u_r, d_r, gu_s, gd_s, gy_s, g_r, h_s, h_r, or_s, or_r, oa_s, oa_r):
    p = lax.axis_index("aux")
    r = lax.axis_index("rep")
    z, y = p // 2, lax.rem(p, 2)
    core = lax.rem(r, 2)
    twin = (p, r + 1 - 2 * core)
    across = (p, lax.rem(r + 2, 4))
    y_peer = (p + 1 - 2 * y, r)
    above = (lax.rem(p + 2, 8), r)
    below = (lax.rem(p + 6, 8), r)
    reps = [(p, lax.rem(r + 1 + s, 4)) for s in range(3)]
    auxes = [(lax.rem(p + 1 + s, 8), r) for s in range(7)]
    width = left.shape[2]
    cols = own.shape[2]
    fetch = pltpu.make_async_copy(left_hbm, left, left_sem)
    fetch.start()
    greet(reps + auxes)

    def place(m):
        first = jnp.where(m == 0, 3, jnp.where(m == 1, 0, jnp.where(m == 2, 2, 1)))
        return first + (z // 2) * (3 - 2 * first)

    def copy_a(k):
        return send(cut.at[k, 1 - core], cut_in.at[k], a_s.at[k], a_r.at[k], twin)

    def copy_b(k):
        return send(chip.at[k], chip_in.at[k], b_s.at[k], b_r.at[k], across)

    def copy_c(k, half):
        return send(block.at[k, half], block.at[k, half], c_s.at[k], c_r.at[k], twin)

    x = r // 2

    def slot_a(t):
        return send(cut.at[2 * t + 1 - core, x], cut_in.at[t], a_s.at[t], a_r.at[t], twin)

    def slot_b(t, side):
        return send(block.at[2 * t + core, side], block.at[2 * t + core, side], b_s.at[t], b_r.at[t], across)

    def slot_c(t, side):
        return send(block.at[2 * t + core, side], block.at[2 * t + core, side], c_s.at[t], c_r.at[t], twin)

    def slot_e(t, side):
        return send(block.at[2 * t + core, side], block.at[2 * t + core, side], e_s.at[t], e_r.at[t], twin)

    def slots_a(m, carry):
        slot_a(place(m)).start()
        return carry

    def slots_b(m, carry):
        t = place(m)
        slot_a(t).wait_recv()
        block[2 * t + core, x] = cut[2 * t + core, x] + cut_in[t]
        slot_b(t, x).start()
        slot_e(t, x).start()
        return carry

    def phase_a(m, carry):
        for u in range(2):
            k = 2 * place(m) + u
            copy_a(k).start()
        return carry

    def phase_b(m, carry):
        for u in range(2):
            k = 2 * place(m) + u
            copy_a(k).wait_recv()
            chip[k] = cut[k, core] + cut_in[k]
            copy_b(k).start()
        return carry

    lax.fori_loop(0, 4, slots_a if one_way else phase_a, 0)
    lax.fori_loop(0, 4, slots_b if one_way else phase_b, 0)
    fetch.wait()

    def copy_y(t):
        return send(y_out.at[t], y_in.at[t], y_s.at[t], y_r.at[t], y_peer)

    def copy_up(t):
        return send(z_out.at[t], up_in.at[t], z_s.at[t], u_r.at[t], above)

    def copy_down(t):
        return send(z_out.at[t], down_in.at[t], z_s.at[t], d_r.at[t], below)

    def gather_sum(t):
        copy_y(t).wait_recv()
        acc[t] = acc[t] + unpack(y_in.at[t])

        @pl.when((z <= t) & (z > 0))
        def _():
            copy_up(t).wait_recv()
            acc[t] = acc[t] + unpack(up_in.at[t])

        @pl.when((z >= t) & (z < 3))
        def _():
            copy_down(t).wait_recv()
            acc[t] = acc[t] + unpack(down_in.at[t])

    def pass_on(t):
        @pl.when(t != z)
        def _():
            gather_sum(t)
            pack(z_out.at[t], acc[t])

        @pl.when(t > z)
        def _():
            copy_up(t).start()

        @pl.when(t < z)
        def _():
            copy_down(t).start()

    def phase_c(m, carry):
        t = place(m)
        if one_way:
            slot_b(t, 1 - x).wait_recv()
            slot_c(t, 1 - x).start()
            slot_e(t, x).wait_recv()
            slot_c(t, 1 - x).wait_recv()
        else:
            for u in range(2):
                k = 2 * t + u
                copy_b(k).wait_recv()
                block[k, core] = chip[k] + chip_in[k]
                copy_c(k, core).start()
        for u in range(2):
            k = 2 * t + (1 - y if u == 0 else y)
            if not one_way:
                copy_c(k, 1 - core).wait_recv()
            for s in range(2):
                part = lax.dot_general(
                    block[k, s], left[2 * k + s], (((0,), (0,)), ((), ())),
                    preferred_element_type=jnp.float32,
                )
                if u == 0:
                    part_out[s * BLK:(s + 1) * BLK, :] = part
                else:
                    acc[t, s * BLK:(s + 1) * BLK, :] = part
            if u == 0:
                pack(y_out.at[t], part_out[...])
                copy_y(t).start()

        @pl.when(m > 0)
        def _():
            pass_on(place(m - 1))

        return carry

    lax.fori_loop(0, 4, phase_c, 0)
    pass_on(place(3))
    gather_sum(z)

    found = jnp.zeros((8, BLK), jnp.float32)
    for s in range(2):
        amplitude = acc[z, s * BLK:(s + 1) * BLK, :] * coef[s * BLK:(s + 1) * BLK, :]
        square = jnp.sum(amplitude * amplitude, axis=0, keepdims=True)
        weight = jnp.sum(square, axis=1, keepdims=True)
        found = found - weight * hits[s]
        amps[p, s * BLK:(s + 1) * BLK, :] = amplitude.astype(jnp.bfloat16)
    occ_rep[r] = found

    def copy_or(s):
        return send(occ_rep.at[r], occ_rep.at[r], or_s.at[s], or_r.at[s], reps[s])

    def copy_oa(s):
        return send(occ_sum, occ_aux.at[p], oa_s.at[s], oa_r.at[s], auxes[s])

    holder = (p * cols) // width
    offset = pl.multiple_of(p * cols - holder * width, BLK)

    def copy_gu(k):
        return send(amps.at[k], amps.at[k], gu_s.at[k], g_r.at[k], above)

    def copy_gd(k):
        return send(amps.at[k], amps.at[k], gd_s.at[k], g_r.at[k], below)

    def copy_gy(k):
        return send(amps.at[k], amps.at[k], gy_s.at[k], g_r.at[k], y_peer)

    def copy_h(k, s):
        return send(amps.at[k, :, pl.ds(offset, cols)], own.at[k], h_s.at[k, s], h_r.at[k], reps[s])

    def share(k):
        @pl.when(r == holder)
        def _():
            for s in range(3):
                copy_h(k, s).start()
            own[k] = amps[k, :, pl.ds(offset, cols)]

    def when_up(k, d, act):
        @pl.when((z < 3) & (d <= 0))
        def _():
            act(copy_gu(k))

    def when_down(k, d, act):
        @pl.when((z > 0) & (d >= 0))
        def _():
            act(copy_gd(k))

    def each(act_fn):
        for d in (0, 1, -1, 2, -2, 3, -3):
            t = z + d

            @pl.when((t >= 0) & (t < 4))
            def _():
                act_fn(t, d)

    def gather(t, d):
        k = 2 * t + y
        if d != 0:
            copy_gy(k).wait_recv()
        when_up(k, d, lambda c: c.start())
        when_down(k, d, lambda c: c.start())
        copy_gy(k).start()
        share(k)

    def gather_y(t, d):
        k = 2 * t + 1 - y
        copy_gy(k).wait_recv()
        share(k)

    def both(t, d):
        gather(t, d)
        if d == 0:
            for s in range(3):
                copy_or(s).start()

    each(both)
    for s in range(3):
        copy_or(s).wait_recv()
    occ_sum[...] = occ_rep[0] + occ_rep[1] + occ_rep[2] + occ_rep[3]
    occ_aux[p] = occ_sum[...]
    for s in range(7):
        copy_oa(s).start()
    each(gather_y)

    @pl.when(r != holder)
    def _():
        for k in range(8):
            copy_h(k, 0).wait_recv()

    dens[...] = lax.dot_general(
        amps[...].reshape(8 * 2 * BLK, width), own[...].reshape(8 * 2 * BLK, cols),
        (((0,), (0,)), ((), ())), preferred_element_type=jnp.float32,
    )
    for s in range(7):
        copy_oa(s).wait_recv()
    total = occ_aux[0]
    for k in range(1, 8):
        total = total + occ_aux[k]
    occ[...] = total

    if not one_way:
        for k in range(8):
            copy_a(k).wait_send()
            copy_b(k).wait_send()
            copy_c(k, core).wait_send()
    for t in range(4):
        if one_way:
            slot_a(t).wait_send()
            slot_b(t, x).wait_send()
            slot_c(t, x).wait_send()
            slot_e(t, x).wait_send()
        copy_y(t).wait_send()

        @pl.when(t != z)
        def _():
            copy_up(t).wait_send()

    def sent(t, d):
        k = 2 * t + y
        when_up(k, d, lambda c: c.wait_send())
        when_down(k, d, lambda c: c.wait_send())
        copy_gy(k).wait_send()

    each(sent)

    @pl.when(r == holder)
    def _():
        for k in range(8):
            for s in range(3):
                copy_h(k, s).wait_send()

    for s in range(3):
        copy_or(s).wait_send()
    for s in range(7):
        copy_oa(s).wait_send()


def local(b_slab, energy_occ, energy_vir, owner, tasks, counts):
    depth, orbs, width = b_slab.shape
    total = energy_vir.shape[0]
    row = jnp.concatenate([tasks.reshape(-1), counts.reshape(-1)])
    row = jnp.broadcast_to(jnp.pad(row, (0, BLK - row.shape[0]))[None], (8, BLK))
    part = 96
    dma = pltpu.SemaphoreType.DMA
    vmem = pl.BlockSpec(memory_space=pltpu.VMEM)
    f32, bf16 = jnp.float32, jnp.bfloat16
    rows = pl.pallas_call(
        spread_rows,
        out_shape=jax.ShapeDtypeStruct((8, 8, BLK), jnp.int32),
        in_specs=[vmem],
        out_specs=vmem,
        scratch_shapes=[
            pltpu.VMEM((8, BLK), jnp.int32), pltpu.VMEM((8, 8, BLK), jnp.int32), dma((7,)), dma((7,)),
        ],
        compiler_params=pltpu.CompilerParams(collective_id=0, has_side_effects=True),
    )(row)
    counts_all = rows[:, 0, 6]
    number = 2 * counts_all.shape[0]
    ids = jnp.arange(number, dtype=jnp.int32)
    side = (rows[:, 0, 2:6:3].reshape(-1) * BLK >= total // 2).astype(jnp.int32)
    alive = (jnp.arange(2, dtype=jnp.int32)[None, :] < counts_all[:, None]).reshape(-1)
    ahead = (ids[:, None] > ids[None, :]) & (side[:, None] == side[None, :]) & alive[None, :]
    rank = jnp.sum(ahead.astype(jnp.int32), axis=1)
    seat = jnp.where(alive, 2 * rank + side, 2 * number)
    one_way = jnp.max(seat * alive) < number
    taken = seat[None, :] == ids[:, None]
    order = jnp.where(one_way, jnp.sum(taken * ids[None, :], axis=1), ids)
    valid = jnp.where(one_way, jnp.sum(taken.astype(jnp.int32), axis=1), alive.astype(jnp.int32))
    left, cut, coef, hits = pl.pallas_call(
        select,
        grid_spec=pltpu.PrefetchScalarGridSpec(
            num_scalar_prefetch=5,
            grid=(depth // part,),
            in_specs=[
                pl.BlockSpec((part, orbs, width), lambda i, *_: (i, 0, 0)),
                pl.BlockSpec((1, total), lambda i, *_: (0, 0)),
                pl.BlockSpec((total, 1), lambda i, *_: (0, 0)),
            ],
            out_specs=(
                pl.BlockSpec((16, part, width), lambda i, *_: (0, i, 0)),
                pl.BlockSpec((8, 2, part, BLK), lambda i, *_: (0, 0, i, 0)),
                pl.BlockSpec((2 * BLK, width), lambda i, *_: (0, 0)),
                pl.BlockSpec((2, 8, BLK), lambda i, *_: (0, 0, 0)),
            ),
            scratch_shapes=[pltpu.VMEM((width // BLK, part * orbs, BLK), f32)],
        ),
        out_shape=(
            jax.ShapeDtypeStruct((16, depth, width), bf16),
            jax.ShapeDtypeStruct((8, 2, depth, BLK), bf16),
            jax.ShapeDtypeStruct((2 * BLK, width), f32),
            jax.ShapeDtypeStruct((2, 8, BLK), f32),
        ),
        compiler_params=pltpu.CompilerParams(vmem_limit_bytes=32 * 2**20),
    )(rows, order, valid, owner, energy_occ, b_slab, energy_vir.reshape(1, -1), energy_vir.reshape(-1, 1))
    cols = total // 8
    call = lambda one_way: pl.pallas_call(
        functools.partial(pairs, one_way),
        out_shape=(
            jax.ShapeDtypeStruct((width, cols), f32),
            jax.ShapeDtypeStruct((8, BLK), f32),
        ),
        in_specs=[vmem, pl.BlockSpec(memory_space=pl.ANY), vmem, vmem],
        out_specs=(vmem, vmem),
        scratch_shapes=[
            pltpu.VMEM((16, depth, width), bf16),
            dma(()),
            pltpu.VMEM((2 * BLK, width), f32),
            pltpu.VMEM((4, 2 * BLK + 16, width), jnp.int16),
            dma((4,)),
            dma((4,)),
            pltpu.VMEM((8, depth, BLK), bf16),
            pltpu.VMEM((8, depth, BLK), bf16),
            pltpu.VMEM((8, depth, BLK), bf16),
            pltpu.VMEM((8, 2, depth, BLK), bf16),
            pltpu.VMEM((4, 2 * BLK + 16, width), jnp.int16),
            pltpu.VMEM((4, 2 * BLK + 16, width), jnp.int16),
            pltpu.VMEM((4, 2 * BLK, width), f32),
            pltpu.VMEM((4, 2 * BLK + 16, width), jnp.int16),
            pltpu.VMEM((4, 2 * BLK + 16, width), jnp.int16),
            pltpu.VMEM((8, 2 * BLK, width), bf16),
            pltpu.VMEM((8, 2 * BLK, cols), bf16),
            pltpu.VMEM((4, 8, BLK), f32),
            pltpu.VMEM((8, 8, BLK), f32),
            pltpu.VMEM((8, BLK), f32),
            dma((8,)), dma((8,)), dma((8,)), dma((8,)), dma((8,)), dma((8,)),
            dma((4,)), dma((4,)), dma((4,)), dma((4,)), dma((4,)),
            dma((8,)), dma((8,)), dma((8,)), dma((8,)),
            dma((8, 3)), dma((8,)),
            dma((3,)), dma((3,)), dma((7,)), dma((7,)),
        ],
        compiler_params=pltpu.CompilerParams(
            collective_id=1 if one_way else 2, has_side_effects=True, vmem_limit_bytes=48 * 2**20
        ),
    )
    density, occupied = lax.cond(one_way, call(True), call(False), cut, left, coef, hits)
    return density, occupied[0, : owner.shape[0]]


def solution(mesh):
    fits = mesh.shape["aux"] == 8 and mesh.shape["rep"] == 4
    return jax.shard_map(
        local if fits else plain,
        mesh=mesh,
        in_specs=(P("aux", None, "rep"), P(), P(), P(), P("aux", None, None), P("aux")),
        out_specs=(P("rep", "aux"), P()),
        check_vma=False,
    )
```

```python
import functools

import jax
import jax.numpy as jnp
from jax import lax
from jax.experimental import pallas as pl
from jax.experimental.pallas import tpu as pltpu
from jax.sharding import PartitionSpec as P

BLK = 128


def plain(b_slab, energy_occ, energy_vir, owner, tasks, counts):
    aux_count = lax.axis_size("aux")
    rep_count = lax.axis_size("rep")
    width = b_slab.shape[2]
    slots = tasks.shape[1]
    occ_total = owner.shape[0]
    occ_local = occ_total // aux_count
    total = energy_vir.shape[0]
    rep_rank = lax.axis_index("rep")
    aux_rank = lax.axis_index("aux")
    rows = jnp.concatenate([tasks.reshape(1, -1), counts.reshape(1, 1)], axis=1)
    rows = lax.all_gather(rows, "aux", axis=0, tiled=True)
    all_tasks = rows[:, :-1].reshape(aux_count, slots, 3)
    base = jnp.arange(aux_count, dtype=jnp.int32)[:, None] * occ_local
    first = owner[base + all_tasks[:, :, 0]].reshape(-1)
    second = owner[base + all_tasks[:, :, 1]].reshape(-1)
    start = all_tasks[:, :, 2].reshape(-1) * BLK
    holder = start // width
    within = start - holder * width
    number = first.shape[0]

    blocks = []
    for t in range(number):
        piece = lax.dynamic_slice(b_slab, (0, second[t], within[t]), (b_slab.shape[0], 1, BLK))[:, 0, :]
        blocks.append(jnp.where(holder[t] == rep_rank, piece, jnp.zeros_like(piece)))
    right = lax.psum(jnp.stack(blocks), "rep")
    left = jnp.take(b_slab, first, axis=1)
    part = jnp.einsum("tpc,pta->tca", right, left, preferred_element_type=jnp.float32)
    coulomb = lax.psum_scatter(part, "aux", scatter_dimension=0, tiled=True)

    mine = lambda v: lax.dynamic_slice_in_dim(v, aux_rank * slots, slots)
    my_first, my_second, my_start = mine(first), mine(second), mine(start)
    quarter = lax.dynamic_slice_in_dim(energy_vir, rep_rank * width, width)
    pair = energy_occ[my_first] + energy_occ[my_second]
    block_energy = jnp.stack([lax.dynamic_slice_in_dim(energy_vir, my_start[t], BLK) for t in range(slots)])
    denominator = pair[:, None, None] - block_energy[:, :, None] - quarter[None, None, :]
    live = jnp.arange(slots, dtype=jnp.int32) < counts[0]
    amplitude = jnp.where(live[:, None, None], coulomb / denominator, jnp.zeros_like(coulomb))
    weight = jnp.sum(amplitude * amplitude, axis=(1, 2))
    orbs = jnp.arange(occ_total, dtype=jnp.int32)
    hits = (my_first[:, None] == orbs).astype(jnp.float32) + (my_second[:, None] == orbs).astype(jnp.float32)
    occupied = lax.psum(-jnp.sum(weight[:, None] * hits, axis=0), ("aux", "rep"))

    amp = amplitude.astype(jnp.bfloat16).reshape(slots * BLK, width)
    amps = lax.all_gather(amp, "aux", axis=0, tiled=True)
    cols = total // aux_count
    where = aux_rank * cols
    own = lax.dynamic_slice_in_dim(amps, lax.rem(where, width), cols, 1)
    own = jnp.where(where // width == rep_rank, own, jnp.zeros_like(own))
    own = lax.psum(own, "rep")
    density = lax.dot_general(amps, own, (((0,), (0,)), ((), ())), preferred_element_type=jnp.float32)
    return density, occupied


MESH = pl.DeviceIdType.MESH


def greet(peers):
    barrier = pltpu.get_barrier_semaphore()
    for peer in peers:
        pl.semaphore_signal(barrier, inc=1, device_id=peer, device_id_type=MESH)
    pl.semaphore_wait(barrier, len(peers))


def send(src, dst, send_sem, recv_sem, peer):
    return pltpu.make_async_remote_copy(
        src_ref=src, dst_ref=dst, send_sem=send_sem, recv_sem=recv_sem, device_id=peer, device_id_type=MESH
    )


def spread_rows(row_ref, rows_ref, mine, landed, rows_send, rows_recv):
    p = lax.axis_index("aux")
    r = lax.axis_index("rep")
    peers = [(lax.rem(p + 1 + s, 8), r) for s in range(7)]
    greet(peers)
    mine[...] = row_ref[...]
    landed[p] = row_ref[...]
    copies = [send(mine, landed.at[p], rows_send.at[s], rows_recv.at[s], peers[s]) for s in range(7)]
    for copy in copies:
        copy.start()
    for copy in copies:
        copy.wait()
    rows_ref[...] = landed[...]


def select(rows, order, valid, owner, e_occ, b_ref, e_row, left, cut, coef, hits, wide):
    p = lax.axis_index("aux")
    r = lax.axis_index("rep")
    depth, orbs, width = b_ref.shape

    def field(k, s, which):
        task = order[2 * k + s]
        return rows[task // 2, 0, 3 * lax.rem(task, 2) + which]

    def orbital(k, s, which):
        return owner[order[2 * k + s] // 2 * 2 + field(k, s, which)]

    wide[...] = jnp.swapaxes(b_ref[...], 0, 1)
    for k in range(8):
        for s in range(2):
            i, j = orbital(k, s, 0), orbital(k, s, 1)
            left[2 * k + s] = wide[i]
            start = field(k, s, 2) * BLK
            holder = start // width
            within = pl.multiple_of(start - holder * width, BLK)
            mask = jnp.full((1, BLK), jnp.where(holder == r, 1.0, 0.0), jnp.float32).astype(jnp.bfloat16)
            cut[k, s] = wide[j, :, pl.ds(within, BLK)] * mask

    @pl.when(pl.program_id(0) == 0)
    def _():
        lanes = lax.broadcasted_iota(jnp.int32, (8, BLK), 1)
        quarter = e_row[:, pl.ds(pl.multiple_of(r * width, BLK), width)]
        for s in range(2):
            i, j = orbital(p, s, 0), orbital(p, s, 1)
            start = pl.multiple_of(field(p, s, 2) * BLK, BLK)
            live = jnp.where(valid[2 * p + s] > 0, 1.0, 0.0)
            column = jnp.broadcast_to(e_row[:, pl.ds(start, BLK)], (BLK, BLK)).T[:, :1]
            denominator = (e_occ[i] + e_occ[j]) - column - quarter
            coef[s * BLK:(s + 1) * BLK, :] = live / denominator
            hits[s] = (lanes == i).astype(jnp.float32) + (lanes == j).astype(jnp.float32)


def pack(dst, x):
    rows = x.shape[0]
    top = jnp.max(jnp.abs(x), axis=0, keepdims=True)
    power = jnp.ceil(jnp.log2(jnp.maximum(top, 1e-30)))
    scaled = jnp.floor(x * jnp.exp2(14.0 - power) + 0.5)
    dst[:rows, :] = scaled.astype(jnp.int32).astype(jnp.int16)
    dst[rows:, :] = jnp.broadcast_to(power, (16, x.shape[1])).astype(jnp.int32).astype(jnp.int16)


def unpack(src):
    rows = src.shape[0] - 16
    power = src[rows:, :].astype(jnp.int32).astype(jnp.float32)[:1]
    return src[:rows, :].astype(jnp.int32).astype(jnp.float32) * jnp.exp2(power - 14.0)


def pairs(one_way, cut, left_hbm, coef, hits, dens, occ,
          left, left_sem, part_out, z_out, e_s, e_r, cut_in, chip, chip_in, block, y_out, y_in, acc, up_in, down_in, amps, own, occ_rep, occ_aux, occ_sum,
          a_s, a_r, b_s, b_r, c_s, c_r, y_s, y_r, z_s, u_r, d_r, gu_s, gd_s, gy_s, g_r, h_s, h_r, or_s, or_r, oa_s, oa_r):
    p = lax.axis_index("aux")
    r = lax.axis_index("rep")
    z, y = p // 2, lax.rem(p, 2)
    core = lax.rem(r, 2)
    twin = (p, r + 1 - 2 * core)
    across = (p, lax.rem(r + 2, 4))
    y_peer = (p + 1 - 2 * y, r)
    above = (lax.rem(p + 2, 8), r)
    below = (lax.rem(p + 6, 8), r)
    reps = [(p, lax.rem(r + 1 + s, 4)) for s in range(3)]
    auxes = [(lax.rem(p + 1 + s, 8), r) for s in range(7)]
    width = left.shape[2]
    cols = own.shape[2]
    fetch = pltpu.make_async_copy(left_hbm, left, left_sem)
    fetch.start()
    greet(reps + auxes)

    def place(m):
        first = jnp.where(m == 0, 3, jnp.where(m == 1, 0, jnp.where(m == 2, 2, 1)))
        return first + (z // 2) * (3 - 2 * first)

    def copy_a(k):
        return send(cut.at[k, 1 - core], cut_in.at[k], a_s.at[k], a_r.at[k], twin)

    def copy_b(k):
        return send(chip.at[k], chip_in.at[k], b_s.at[k], b_r.at[k], across)

    def copy_c(k, half):
        return send(block.at[k, half], block.at[k, half], c_s.at[k], c_r.at[k], twin)

    x = r // 2

    def slot_a(t):
        return send(cut.at[2 * t + 1 - core, x], cut_in.at[t], a_s.at[t], a_r.at[t], twin)

    def slot_b(t, side):
        return send(block.at[2 * t + core, side], block.at[2 * t + core, side], b_s.at[t], b_r.at[t], across)

    def slot_c(t, side):
        return send(block.at[2 * t + core, side], block.at[2 * t + core, side], c_s.at[t], c_r.at[t], twin)

    def slot_e(t, side):
        return send(block.at[2 * t + core, side], block.at[2 * t + core, side], e_s.at[t], e_r.at[t], twin)

    def slots_a(m, carry):
        slot_a(place(m)).start()
        return carry

    def slots_b(m, carry):
        t = place(m)
        slot_a(t).wait_recv()
        block[2 * t + core, x] = cut[2 * t + core, x] + cut_in[t]
        slot_b(t, x).start()
        slot_e(t, x).start()
        return carry

    def phase_a(m, carry):
        for u in range(2):
            k = 2 * place(m) + u
            copy_a(k).start()
        return carry

    def phase_b(m, carry):
        for u in range(2):
            k = 2 * place(m) + u
            copy_a(k).wait_recv()
            chip[k] = cut[k, core] + cut_in[k]
            copy_b(k).start()
        return carry

    lax.fori_loop(0, 4, slots_a if one_way else phase_a, 0)
    lax.fori_loop(0, 4, slots_b if one_way else phase_b, 0)
    fetch.wait()

    def copy_y(t):
        return send(y_out.at[t], y_in.at[t], y_s.at[t], y_r.at[t], y_peer)

    def copy_up(t):
        return send(z_out.at[t], up_in.at[t], z_s.at[t], u_r.at[t], above)

    def copy_down(t):
        return send(z_out.at[t], down_in.at[t], z_s.at[t], d_r.at[t], below)

    def gather_sum(t):
        copy_y(t).wait_recv()
        acc[t] = acc[t] + unpack(y_in.at[t])

        @pl.when((z <= t) & (z > 0))
        def _():
            copy_up(t).wait_recv()
            acc[t] = acc[t] + unpack(up_in.at[t])

        @pl.when((z >= t) & (z < 3))
        def _():
            copy_down(t).wait_recv()
            acc[t] = acc[t] + unpack(down_in.at[t])

    def pass_on(t):
        @pl.when(t != z)
        def _():
            gather_sum(t)
            pack(z_out.at[t], acc[t])

        @pl.when(t > z)
        def _():
            copy_up(t).start()

        @pl.when(t < z)
        def _():
            copy_down(t).start()

    def phase_c(m, carry):
        t = place(m)
        if one_way:
            slot_b(t, 1 - x).wait_recv()
            slot_c(t, 1 - x).start()
            slot_e(t, x).wait_recv()
            slot_c(t, 1 - x).wait_recv()
        else:
            for u in range(2):
                k = 2 * t + u
                copy_b(k).wait_recv()
                block[k, core] = chip[k] + chip_in[k]
                copy_c(k, core).start()
        for u in range(2):
            k = 2 * t + (1 - y if u == 0 else y)
            if not one_way:
                copy_c(k, 1 - core).wait_recv()
            for s in range(2):
                part = lax.dot_general(
                    block[k, s], left[2 * k + s], (((0,), (0,)), ((), ())),
                    preferred_element_type=jnp.float32,
                )
                if u == 0:
                    part_out[s * BLK:(s + 1) * BLK, :] = part
                else:
                    acc[t, s * BLK:(s + 1) * BLK, :] = part
            if u == 0:
                pack(y_out.at[t], part_out[...])
                copy_y(t).start()

        @pl.when(m > 0)
        def _():
            pass_on(place(m - 1))

        return carry

    lax.fori_loop(0, 4, phase_c, 0)
    pass_on(place(3))
    gather_sum(z)

    found = jnp.zeros((8, BLK), jnp.float32)
    for s in range(2):
        amplitude = acc[z, s * BLK:(s + 1) * BLK, :] * coef[s * BLK:(s + 1) * BLK, :]
        square = jnp.sum(amplitude * amplitude, axis=0, keepdims=True)
        weight = jnp.sum(square, axis=1, keepdims=True)
        found = found - weight * hits[s]
        amps[p, s * BLK:(s + 1) * BLK, :] = amplitude.astype(jnp.bfloat16)
    occ_rep[r] = found

    def copy_or(s):
        return send(occ_rep.at[r], occ_rep.at[r], or_s.at[s], or_r.at[s], reps[s])

    def copy_oa(s):
        return send(occ_sum, occ_aux.at[p], oa_s.at[s], oa_r.at[s], auxes[s])

    holder = (p * cols) // width
    offset = pl.multiple_of(p * cols - holder * width, BLK)

    def copy_gu(k):
        return send(amps.at[k], amps.at[k], gu_s.at[k], g_r.at[k], above)

    def copy_gd(k):
        return send(amps.at[k], amps.at[k], gd_s.at[k], g_r.at[k], below)

    def copy_gy(k):
        return send(amps.at[k], amps.at[k], gy_s.at[k], g_r.at[k], y_peer)

    def copy_h(k, s):
        return send(amps.at[k, :, pl.ds(offset, cols)], own.at[k], h_s.at[k, s], h_r.at[k], reps[s])

    def share(k):
        @pl.when(r == holder)
        def _():
            for s in range(3):
                copy_h(k, s).start()
            own[k] = amps[k, :, pl.ds(offset, cols)]

    def when_up(k, d, act):
        @pl.when((z < 3) & (d <= 0))
        def _():
            act(copy_gu(k))

    def when_down(k, d, act):
        @pl.when((z > 0) & (d >= 0))
        def _():
            act(copy_gd(k))

    def at(act_fn, *offsets):
        for d in offsets:
            t = z + d

            @pl.when((t >= 0) & (t < 4))
            def _():
                act_fn(t, d)

    def gather(t, d):
        k = 2 * t + y
        if d != 0:
            copy_gy(k).wait_recv()
        when_up(k, d, lambda c: c.start())
        when_down(k, d, lambda c: c.start())
        copy_gy(k).start()
        share(k)

    def gather_y(t, d):
        k = 2 * t + 1 - y
        copy_gy(k).wait_recv()
        share(k)

    def multiply(t, d):
        @pl.when(r != holder)
        def _():
            for u in range(2):
                copy_h(2 * t + u, 0).wait_recv()

        more = lax.dot_general(
            amps[pl.ds(2 * t, 2)].reshape(4 * BLK, width), own[pl.ds(2 * t, 2)].reshape(4 * BLK, cols),
            (((0,), (0,)), ((), ())), preferred_element_type=jnp.float32,
        )
        dens[...] = more if d == 0 else dens[...] + more

    at(gather, 0)
    for s in range(3):
        copy_or(s).start()
    at(gather, 1, -1)
    at(gather_y, 0)
    for s in range(3):
        copy_or(s).wait_recv()
    occ_sum[...] = occ_rep[0] + occ_rep[1] + occ_rep[2] + occ_rep[3]
    occ_aux[p] = occ_sum[...]
    for s in range(7):
        copy_oa(s).start()
    at(gather, 2, -2)
    at(gather_y, 1)
    at(multiply, 0)
    at(gather, 3, -3)
    at(gather_y, -1)
    at(multiply, 1)
    at(gather_y, 2)
    at(multiply, -1)
    at(gather_y, -2)
    at(multiply, 2)
    at(gather_y, 3)
    at(multiply, -2)
    at(gather_y, -3)
    at(multiply, 3, -3)
    for s in range(7):
        copy_oa(s).wait_recv()
    total = occ_aux[0]
    for k in range(1, 8):
        total = total + occ_aux[k]
    occ[...] = total

    if not one_way:
        for k in range(8):
            copy_a(k).wait_send()
            copy_b(k).wait_send()
            copy_c(k, core).wait_send()
    for t in range(4):
        if one_way:
            slot_a(t).wait_send()
            slot_b(t, x).wait_send()
            slot_c(t, x).wait_send()
            slot_e(t, x).wait_send()
        copy_y(t).wait_send()

        @pl.when(t != z)
        def _():
            copy_up(t).wait_send()

    def sent(t, d):
        k = 2 * t + y
        when_up(k, d, lambda c: c.wait_send())
        when_down(k, d, lambda c: c.wait_send())
        copy_gy(k).wait_send()

    at(sent, 0, 1, -1, 2, -2, 3, -3)

    @pl.when(r == holder)
    def _():
        for k in range(8):
            for s in range(3):
                copy_h(k, s).wait_send()

    for s in range(3):
        copy_or(s).wait_send()
    for s in range(7):
        copy_oa(s).wait_send()


def local(b_slab, energy_occ, energy_vir, owner, tasks, counts):
    depth, orbs, width = b_slab.shape
    total = energy_vir.shape[0]
    row = jnp.concatenate([tasks.reshape(-1), counts.reshape(-1)])
    row = jnp.broadcast_to(jnp.pad(row, (0, BLK - row.shape[0]))[None], (8, BLK))
    part = 96
    dma = pltpu.SemaphoreType.DMA
    vmem = pl.BlockSpec(memory_space=pltpu.VMEM)
    f32, bf16 = jnp.float32, jnp.bfloat16
    rows = pl.pallas_call(
        spread_rows,
        out_shape=jax.ShapeDtypeStruct((8, 8, BLK), jnp.int32),
        in_specs=[vmem],
        out_specs=vmem,
        scratch_shapes=[
            pltpu.VMEM((8, BLK), jnp.int32), pltpu.VMEM((8, 8, BLK), jnp.int32), dma((7,)), dma((7,)),
        ],
        compiler_params=pltpu.CompilerParams(collective_id=0, has_side_effects=True),
    )(row)
    counts_all = rows[:, 0, 6]
    number = 2 * counts_all.shape[0]
    ids = jnp.arange(number, dtype=jnp.int32)
    side = (rows[:, 0, 2:6:3].reshape(-1) * BLK >= total // 2).astype(jnp.int32)
    alive = (jnp.arange(2, dtype=jnp.int32)[None, :] < counts_all[:, None]).reshape(-1)
    ahead = (ids[:, None] > ids[None, :]) & (side[:, None] == side[None, :]) & alive[None, :]
    rank = jnp.sum(ahead.astype(jnp.int32), axis=1)
    seat = jnp.where(alive, 2 * rank + side, 2 * number)
    one_way = jnp.max(seat * alive) < number
    taken = seat[None, :] == ids[:, None]
    order = jnp.where(one_way, jnp.sum(taken * ids[None, :], axis=1), ids)
    valid = jnp.where(one_way, jnp.sum(taken.astype(jnp.int32), axis=1), alive.astype(jnp.int32))
    left, cut, coef, hits = pl.pallas_call(
        select,
        grid_spec=pltpu.PrefetchScalarGridSpec(
            num_scalar_prefetch=5,
            grid=(depth // part,),
            in_specs=[
                pl.BlockSpec((part, orbs, width), lambda i, *_: (i, 0, 0)),
                pl.BlockSpec((1, total), lambda i, *_: (0, 0)),
            ],
            out_specs=(
                pl.BlockSpec((16, part, width), lambda i, *_: (0, i, 0)),
                pl.BlockSpec((8, 2, part, BLK), lambda i, *_: (0, 0, i, 0)),
                pl.BlockSpec((2 * BLK, width), lambda i, *_: (0, 0)),
                pl.BlockSpec((2, 8, BLK), lambda i, *_: (0, 0, 0)),
            ),
            scratch_shapes=[pltpu.VMEM((orbs, part, width), bf16)],
        ),
        out_shape=(
            jax.ShapeDtypeStruct((16, depth, width), bf16),
            jax.ShapeDtypeStruct((8, 2, depth, BLK), bf16),
            jax.ShapeDtypeStruct((2 * BLK, width), f32),
            jax.ShapeDtypeStruct((2, 8, BLK), f32),
        ),
        compiler_params=pltpu.CompilerParams(vmem_limit_bytes=58 * 2**20),
    )(rows, order, valid, owner, energy_occ, b_slab, energy_vir.reshape(1, -1))
    cols = total // 8
    call = lambda one_way: pl.pallas_call(
        functools.partial(pairs, one_way),
        out_shape=(
            jax.ShapeDtypeStruct((width, cols), f32),
            jax.ShapeDtypeStruct((8, BLK), f32),
        ),
        in_specs=[vmem, pl.BlockSpec(memory_space=pl.ANY), vmem, vmem],
        out_specs=(vmem, vmem),
        scratch_shapes=[
            pltpu.VMEM((16, depth, width), bf16),
            dma(()),
            pltpu.VMEM((2 * BLK, width), f32),
            pltpu.VMEM((4, 2 * BLK + 16, width), jnp.int16),
            dma((4,)),
            dma((4,)),
            pltpu.VMEM((8, depth, BLK), bf16),
            pltpu.VMEM((8, depth, BLK), bf16),
            pltpu.VMEM((8, depth, BLK), bf16),
            pltpu.VMEM((8, 2, depth, BLK), bf16),
            pltpu.VMEM((4, 2 * BLK + 16, width), jnp.int16),
            pltpu.VMEM((4, 2 * BLK + 16, width), jnp.int16),
            pltpu.VMEM((4, 2 * BLK, width), f32),
            pltpu.VMEM((4, 2 * BLK + 16, width), jnp.int16),
            pltpu.VMEM((4, 2 * BLK + 16, width), jnp.int16),
            pltpu.VMEM((8, 2 * BLK, width), bf16),
            pltpu.VMEM((8, 2 * BLK, cols), bf16),
            pltpu.VMEM((4, 8, BLK), f32),
            pltpu.VMEM((8, 8, BLK), f32),
            pltpu.VMEM((8, BLK), f32),
            dma((8,)), dma((8,)), dma((8,)), dma((8,)), dma((8,)), dma((8,)),
            dma((4,)), dma((4,)), dma((4,)), dma((4,)), dma((4,)),
            dma((8,)), dma((8,)), dma((8,)), dma((8,)),
            dma((8, 3)), dma((8,)),
            dma((3,)), dma((3,)), dma((7,)), dma((7,)),
        ],
        compiler_params=pltpu.CompilerParams(
            collective_id=1 if one_way else 2, has_side_effects=True, vmem_limit_bytes=48 * 2**20
        ),
    )
    density, occupied = lax.cond(one_way, call(True), call(False), cut, left, coef, hits)
    return density, occupied[0, : owner.shape[0]]


def solution(mesh):
    fits = mesh.shape["aux"] == 8 and mesh.shape["rep"] == 4
    return jax.shard_map(
        local if fits else plain,
        mesh=mesh,
        in_specs=(P("aux", None, "rep"), P(), P(), P(), P("aux", None, None), P("aux")),
        out_specs=(P("rep", "aux"), P()),
        check_vma=False,
    )
```

```python
import functools

import jax
import jax.numpy as jnp
from jax import lax
from jax.experimental import pallas as pl
from jax.experimental.pallas import tpu as pltpu
from jax.sharding import PartitionSpec as P

BLK = 128


def plain(b_slab, energy_occ, energy_vir, owner, tasks, counts):
    aux_count = lax.axis_size("aux")
    rep_count = lax.axis_size("rep")
    width = b_slab.shape[2]
    slots = tasks.shape[1]
    occ_total = owner.shape[0]
    occ_local = occ_total // aux_count
    total = energy_vir.shape[0]
    rep_rank = lax.axis_index("rep")
    aux_rank = lax.axis_index("aux")
    rows = jnp.concatenate([tasks.reshape(1, -1), counts.reshape(1, 1)], axis=1)
    rows = lax.all_gather(rows, "aux", axis=0, tiled=True)
    all_tasks = rows[:, :-1].reshape(aux_count, slots, 3)
    base = jnp.arange(aux_count, dtype=jnp.int32)[:, None] * occ_local
    first = owner[base + all_tasks[:, :, 0]].reshape(-1)
    second = owner[base + all_tasks[:, :, 1]].reshape(-1)
    start = all_tasks[:, :, 2].reshape(-1) * BLK
    holder = start // width
    within = start - holder * width
    number = first.shape[0]

    blocks = []
    for t in range(number):
        piece = lax.dynamic_slice(b_slab, (0, second[t], within[t]), (b_slab.shape[0], 1, BLK))[:, 0, :]
        blocks.append(jnp.where(holder[t] == rep_rank, piece, jnp.zeros_like(piece)))
    right = lax.psum(jnp.stack(blocks), "rep")
    left = jnp.take(b_slab, first, axis=1)
    part = jnp.einsum("tpc,pta->tca", right, left, preferred_element_type=jnp.float32)
    coulomb = lax.psum_scatter(part, "aux", scatter_dimension=0, tiled=True)

    mine = lambda v: lax.dynamic_slice_in_dim(v, aux_rank * slots, slots)
    my_first, my_second, my_start = mine(first), mine(second), mine(start)
    quarter = lax.dynamic_slice_in_dim(energy_vir, rep_rank * width, width)
    pair = energy_occ[my_first] + energy_occ[my_second]
    block_energy = jnp.stack([lax.dynamic_slice_in_dim(energy_vir, my_start[t], BLK) for t in range(slots)])
    denominator = pair[:, None, None] - block_energy[:, :, None] - quarter[None, None, :]
    live = jnp.arange(slots, dtype=jnp.int32) < counts[0]
    amplitude = jnp.where(live[:, None, None], coulomb / denominator, jnp.zeros_like(coulomb))
    weight = jnp.sum(amplitude * amplitude, axis=(1, 2))
    orbs = jnp.arange(occ_total, dtype=jnp.int32)
    hits = (my_first[:, None] == orbs).astype(jnp.float32) + (my_second[:, None] == orbs).astype(jnp.float32)
    occupied = lax.psum(-jnp.sum(weight[:, None] * hits, axis=0), ("aux", "rep"))

    amp = amplitude.astype(jnp.bfloat16).reshape(slots * BLK, width)
    amps = lax.all_gather(amp, "aux", axis=0, tiled=True)
    cols = total // aux_count
    where = aux_rank * cols
    own = lax.dynamic_slice_in_dim(amps, lax.rem(where, width), cols, 1)
    own = jnp.where(where // width == rep_rank, own, jnp.zeros_like(own))
    own = lax.psum(own, "rep")
    density = lax.dot_general(amps, own, (((0,), (0,)), ((), ())), preferred_element_type=jnp.float32)
    return density, occupied


MESH = pl.DeviceIdType.MESH


def greet(peers):
    barrier = pltpu.get_barrier_semaphore()
    for peer in peers:
        pl.semaphore_signal(barrier, inc=1, device_id=peer, device_id_type=MESH)
    pl.semaphore_wait(barrier, len(peers))


def send(src, dst, send_sem, recv_sem, peer):
    return pltpu.make_async_remote_copy(
        src_ref=src, dst_ref=dst, send_sem=send_sem, recv_sem=recv_sem, device_id=peer, device_id_type=MESH
    )


def spread_rows(row_ref, rows_ref, mine, landed, rows_send, rows_recv):
    p = lax.axis_index("aux")
    r = lax.axis_index("rep")
    peers = [(lax.rem(p + 1 + s, 8), r) for s in range(7)]
    greet(peers)
    mine[...] = row_ref[...]
    landed[p] = row_ref[...]
    copies = [send(mine, landed.at[p], rows_send.at[s], rows_recv.at[s], peers[s]) for s in range(7)]
    for copy in copies:
        copy.start()
    for copy in copies:
        copy.wait()
    rows_ref[...] = landed[...]


def select(rows, order, valid, owner, e_occ, b_ref, e_row, left, cut, coef, hits, wide):
    p = lax.axis_index("aux")
    r = lax.axis_index("rep")
    depth, orbs, width = b_ref.shape

    def field(k, s, which):
        task = order[2 * k + s]
        return rows[task // 2, 0, 3 * lax.rem(task, 2) + which]

    def orbital(k, s, which):
        return owner[order[2 * k + s] // 2 * 2 + field(k, s, which)]

    wide[...] = jnp.swapaxes(b_ref[...], 0, 1)
    for k in range(8):
        for s in range(2):
            i, j = orbital(k, s, 0), orbital(k, s, 1)
            left[2 * k + s] = wide[i]
            start = field(k, s, 2) * BLK
            holder = start // width
            within = pl.multiple_of(start - holder * width, BLK)
            mask = jnp.full((1, BLK), jnp.where(holder == r, 1.0, 0.0), jnp.float32).astype(jnp.bfloat16)
            cut[k, s] = wide[j, :, pl.ds(within, BLK)] * mask

    @pl.when(pl.program_id(0) == 0)
    def _():
        lanes = lax.broadcasted_iota(jnp.int32, (8, BLK), 1)
        quarter = e_row[:, pl.ds(pl.multiple_of(r * width, BLK), width)]
        for s in range(2):
            i, j = orbital(p, s, 0), orbital(p, s, 1)
            start = pl.multiple_of(field(p, s, 2) * BLK, BLK)
            live = jnp.where(valid[2 * p + s] > 0, 1.0, 0.0)
            column = jnp.broadcast_to(e_row[:, pl.ds(start, BLK)], (BLK, BLK)).T[:, :1]
            denominator = (e_occ[i] + e_occ[j]) - column - quarter
            coef[s * BLK:(s + 1) * BLK, :] = live / denominator
            hits[s] = (lanes == i).astype(jnp.float32) + (lanes == j).astype(jnp.float32)


def pack(dst, x):
    rows = x.shape[0]
    top = jnp.max(jnp.abs(x), axis=0, keepdims=True)
    power = jnp.ceil(jnp.log2(jnp.maximum(top, 1e-30)))
    scaled = jnp.floor(x * jnp.exp2(14.0 - power) + 0.5)
    dst[:rows, :] = scaled.astype(jnp.int32).astype(jnp.int16)
    dst[rows:, :] = jnp.broadcast_to(power, (16, x.shape[1])).astype(jnp.int32).astype(jnp.int16)


def unpack(src):
    rows = src.shape[0] - 16
    power = src[rows:, :].astype(jnp.int32).astype(jnp.float32)[:1]
    return src[:rows, :].astype(jnp.int32).astype(jnp.float32) * jnp.exp2(power - 14.0)


def pairs(one_way, cut, left_hbm, coef, hits, dens, occ,
          left, left_sem, z_out, e_s, e_r, cut_in, chip, chip_in, block, y_out, y_in, acc, up_in, down_in, amps, own, occ_rep, occ_aux, occ_sum,
          a_s, a_r, b_s, b_r, c_s, c_r, y_s, y_r, z_s, u_r, d_r, gu_s, gd_s, gy_s, g_r, h_s, h_r, or_s, or_r, oa_s, oa_r):
    p = lax.axis_index("aux")
    r = lax.axis_index("rep")
    z, y = p // 2, lax.rem(p, 2)
    core = lax.rem(r, 2)
    twin = (p, r + 1 - 2 * core)
    across = (p, lax.rem(r + 2, 4))
    y_peer = (p + 1 - 2 * y, r)
    above = (lax.rem(p + 2, 8), r)
    below = (lax.rem(p + 6, 8), r)
    reps = [(p, lax.rem(r + 1 + s, 4)) for s in range(3)]
    auxes = [(lax.rem(p + 1 + s, 8), r) for s in range(7)]
    width = left.shape[2]
    cols = own.shape[2]
    fetch = pltpu.make_async_copy(left_hbm, left, left_sem)
    fetch.start()
    greet(reps + auxes)

    def place(m):
        first = jnp.where(m == 0, 3, jnp.where(m == 1, 0, jnp.where(m == 2, 2, 1)))
        return first + (z // 2) * (3 - 2 * first)

    def copy_a(k):
        return send(cut.at[k, 1 - core], cut_in.at[k], a_s.at[k], a_r.at[k], twin)

    def copy_b(k):
        return send(chip.at[k], chip_in.at[k], b_s.at[k], b_r.at[k], across)

    def copy_c(k, half):
        return send(block.at[k, half], block.at[k, half], c_s.at[k], c_r.at[k], twin)

    x = r // 2

    def slot_a(t):
        return send(cut.at[2 * t + 1 - core, x], cut_in.at[t], a_s.at[t], a_r.at[t], twin)

    def slot_b(t, side):
        return send(block.at[2 * t + core, side], block.at[2 * t + core, side], b_s.at[t], b_r.at[t], across)

    def slot_c(t, side):
        return send(block.at[2 * t + core, side], block.at[2 * t + core, side], c_s.at[t], c_r.at[t], twin)

    def slot_e(t, side):
        return send(block.at[2 * t + core, side], block.at[2 * t + core, side], e_s.at[t], e_r.at[t], twin)

    def slots_a(m, carry):
        slot_a(place(m)).start()
        return carry

    def slots_b(m, carry):
        t = place(m)
        slot_a(t).wait_recv()
        block[2 * t + core, x] = cut[2 * t + core, x] + cut_in[t]
        slot_b(t, x).start()
        slot_e(t, x).start()
        return carry

    def phase_a(m, carry):
        for u in range(2):
            k = 2 * place(m) + u
            copy_a(k).start()
        return carry

    def phase_b(m, carry):
        for u in range(2):
            k = 2 * place(m) + u
            copy_a(k).wait_recv()
            chip[k] = cut[k, core] + cut_in[k]
            copy_b(k).start()
        return carry

    lax.fori_loop(0, 4, slots_a if one_way else phase_a, 0)
    lax.fori_loop(0, 4, slots_b if one_way else phase_b, 0)
    fetch.wait()

    def copy_y(t, s):
        return send(y_out.at[t, s], y_in.at[t, s], y_s.at[t, s], y_r.at[t, s], y_peer)

    def copy_up(t):
        return send(z_out.at[t], up_in.at[t], z_s.at[t], u_r.at[t], above)

    def copy_down(t):
        return send(z_out.at[t], down_in.at[t], z_s.at[t], d_r.at[t], below)

    def gather_sum(t):
        for s in range(2):
            copy_y(t, s).wait_recv()
            acc[t, s] = acc[t, s] + unpack(y_in.at[t, s])

        @pl.when((z <= t) & (z > 0))
        def _():
            copy_up(t).wait_recv()
            acc[t] = acc[t] + unpack(up_in.at[t]).reshape(2, BLK, width)

        @pl.when((z >= t) & (z < 3))
        def _():
            copy_down(t).wait_recv()
            acc[t] = acc[t] + unpack(down_in.at[t]).reshape(2, BLK, width)

    def pass_on(t):
        @pl.when(t != z)
        def _():
            gather_sum(t)
            pack(z_out.at[t], acc[t].reshape(2 * BLK, width))

        @pl.when(t > z)
        def _():
            copy_up(t).start()

        @pl.when(t < z)
        def _():
            copy_down(t).start()

    def product(k, s):
        return lax.dot_general(
            block[k, s], left[2 * k + s], (((0,), (0,)), ((), ())), preferred_element_type=jnp.float32
        )

    def partial(t, s):
        pack(y_out.at[t, s], product(2 * t + 1 - y, s))
        copy_y(t, s).start()
        acc[t, s] = product(2 * t + y, s)

    def near(m, carry):
        t = place(m)
        slot_e(t, x).wait_recv()
        partial(t, x)
        return carry

    if one_way:
        lax.fori_loop(0, 4, near, 0)

    def phase_c(m, carry):
        t = place(m)
        if one_way:
            slot_b(t, 1 - x).wait_recv()
            slot_c(t, 1 - x).start()
            slot_c(t, 1 - x).wait_recv()
            partial(t, 1 - x)
        else:
            for u in range(2):
                k = 2 * t + u
                copy_b(k).wait_recv()
                block[k, core] = chip[k] + chip_in[k]
                copy_c(k, core).start()
            for u in range(2):
                copy_c(2 * t + u, 1 - core).wait_recv()
            for s in range(2):
                partial(t, s)

        @pl.when(m > 0)
        def _():
            pass_on(place(m - 1))

        return carry

    lax.fori_loop(0, 4, phase_c, 0)
    pass_on(place(3))
    gather_sum(z)

    found = jnp.zeros((8, BLK), jnp.float32)
    for s in range(2):
        amplitude = acc[z, s] * coef[s * BLK:(s + 1) * BLK, :]
        square = jnp.sum(amplitude * amplitude, axis=0, keepdims=True)
        weight = jnp.sum(square, axis=1, keepdims=True)
        found = found - weight * hits[s]
        amps[p, s * BLK:(s + 1) * BLK, :] = amplitude.astype(jnp.bfloat16)
    occ_rep[r] = found

    def copy_or(s):
        return send(occ_rep.at[r], occ_rep.at[r], or_s.at[s], or_r.at[s], reps[s])

    def copy_oa(s):
        return send(occ_sum, occ_aux.at[p], oa_s.at[s], oa_r.at[s], auxes[s])

    holder = (p * cols) // width
    offset = pl.multiple_of(p * cols - holder * width, BLK)

    def copy_gu(k):
        return send(amps.at[k], amps.at[k], gu_s.at[k], g_r.at[k], above)

    def copy_gd(k):
        return send(amps.at[k], amps.at[k], gd_s.at[k], g_r.at[k], below)

    def copy_gy(k):
        return send(amps.at[k], amps.at[k], gy_s.at[k], g_r.at[k], y_peer)

    relay = r == lax.rem(holder + 2, 4)

    def copy_h(k, s):
        return send(amps.at[k, :, pl.ds(offset, cols)], own.at[k], h_s.at[k, s], h_r.at[k], (twin, across)[s])

    def copy_relay(k):
        return send(own.at[k], own.at[k], h_s.at[k, 0], h_r.at[k], twin)

    def share(k):
        @pl.when(r == holder)
        def _():
            copy_h(k, 1).start()
            copy_h(k, 0).start()
            own[k] = amps[k, :, pl.ds(offset, cols)]

    def when_up(k, d, act):
        @pl.when((z < 3) & (d <= 0))
        def _():
            act(copy_gu(k))

    def when_down(k, d, act):
        @pl.when((z > 0) & (d >= 0))
        def _():
            act(copy_gd(k))

    def at(act_fn, *offsets):
        for d in offsets:
            t = z + d

            @pl.when((t >= 0) & (t < 4))
            def _():
                act_fn(t, d)

    def gather(t, d):
        k = 2 * t + y
        if d != 0:
            copy_gy(k).wait_recv()
        when_up(k, d, lambda c: c.start())
        when_down(k, d, lambda c: c.start())
        copy_gy(k).start()
        share(k)

    def gather_y(t, d):
        k = 2 * t + 1 - y
        copy_gy(k).wait_recv()
        share(k)

    def multiply(t, d):
        @pl.when(r != holder)
        def _():
            for u in range(2):
                copy_h(2 * t + u, 0).wait_recv()

                @pl.when(relay)
                def _():
                    copy_relay(2 * t + u).start()

        more = lax.dot_general(
            amps[pl.ds(2 * t, 2)].reshape(4 * BLK, width), own[pl.ds(2 * t, 2)].reshape(4 * BLK, cols),
            (((0,), (0,)), ((), ())), preferred_element_type=jnp.float32,
        )
        dens[...] = more if d == 0 else dens[...] + more

    at(gather, 0)
    for s in range(3):
        copy_or(s).start()
    at(gather, 1, -1)
    at(gather_y, 0)
    for s in range(3):
        copy_or(s).wait_recv()
    occ_sum[...] = occ_rep[0] + occ_rep[1] + occ_rep[2] + occ_rep[3]
    occ_aux[p] = occ_sum[...]
    for s in range(7):
        copy_oa(s).start()
    at(gather, 2, -2)
    at(gather_y, 1)
    at(multiply, 0)
    at(gather, 3, -3)
    at(gather_y, -1)
    at(multiply, 1)
    at(gather_y, 2)
    at(multiply, -1)
    at(gather_y, -2)
    at(multiply, 2)
    at(gather_y, 3)
    at(multiply, -2)
    at(gather_y, -3)
    at(multiply, 3, -3)
    for s in range(7):
        copy_oa(s).wait_recv()
    total = occ_aux[0]
    for k in range(1, 8):
        total = total + occ_aux[k]
    occ[...] = total

    if not one_way:
        for k in range(8):
            copy_a(k).wait_send()
            copy_b(k).wait_send()
            copy_c(k, core).wait_send()
    for t in range(4):
        if one_way:
            slot_a(t).wait_send()
            slot_b(t, x).wait_send()
            slot_c(t, x).wait_send()
            slot_e(t, x).wait_send()
        for s in range(2):
            copy_y(t, s).wait_send()

        @pl.when(t != z)
        def _():
            copy_up(t).wait_send()

    def sent(t, d):
        k = 2 * t + y
        when_up(k, d, lambda c: c.wait_send())
        when_down(k, d, lambda c: c.wait_send())
        copy_gy(k).wait_send()

    at(sent, 0, 1, -1, 2, -2, 3, -3)

    @pl.when(r == holder)
    def _():
        for k in range(8):
            for s in range(2):
                copy_h(k, s).wait_send()

    @pl.when(relay)
    def _():
        for k in range(8):
            copy_relay(k).wait_send()

    for s in range(3):
        copy_or(s).wait_send()
    for s in range(7):
        copy_oa(s).wait_send()


def local(b_slab, energy_occ, energy_vir, owner, tasks, counts):
    depth, orbs, width = b_slab.shape
    total = energy_vir.shape[0]
    row = jnp.concatenate([tasks.reshape(-1), counts.reshape(-1)])
    row = jnp.broadcast_to(jnp.pad(row, (0, BLK - row.shape[0]))[None], (8, BLK))
    part = 192
    dma = pltpu.SemaphoreType.DMA
    vmem = pl.BlockSpec(memory_space=pltpu.VMEM)
    f32, bf16 = jnp.float32, jnp.bfloat16
    rows = pl.pallas_call(
        spread_rows,
        out_shape=jax.ShapeDtypeStruct((8, 8, BLK), jnp.int32),
        in_specs=[vmem],
        out_specs=vmem,
        scratch_shapes=[
            pltpu.VMEM((8, BLK), jnp.int32), pltpu.VMEM((8, 8, BLK), jnp.int32), dma((7,)), dma((7,)),
        ],
        compiler_params=pltpu.CompilerParams(collective_id=0, has_side_effects=True),
    )(row)
    counts_all = rows[:, 0, 6]
    number = 2 * counts_all.shape[0]
    ids = jnp.arange(number, dtype=jnp.int32)
    side = (rows[:, 0, 2:6:3].reshape(-1) * BLK >= total // 2).astype(jnp.int32)
    alive = (jnp.arange(2, dtype=jnp.int32)[None, :] < counts_all[:, None]).reshape(-1)
    ahead = (ids[:, None] > ids[None, :]) & (side[:, None] == side[None, :]) & alive[None, :]
    rank = jnp.sum(ahead.astype(jnp.int32), axis=1)
    seat = jnp.where(alive, 2 * rank + side, 2 * number)
    one_way = jnp.max(seat * alive) < number
    taken = seat[None, :] == ids[:, None]
    order = jnp.where(one_way, jnp.sum(taken * ids[None, :], axis=1), ids)
    valid = jnp.where(one_way, jnp.sum(taken.astype(jnp.int32), axis=1), alive.astype(jnp.int32))
    left, cut, coef, hits = pl.pallas_call(
        select,
        grid_spec=pltpu.PrefetchScalarGridSpec(
            num_scalar_prefetch=5,
            grid=(depth // part,),
            in_specs=[
                pl.BlockSpec((part, orbs, width), lambda i, *_: (i, 0, 0)),
                pl.BlockSpec((1, total), lambda i, *_: (0, 0)),
            ],
            out_specs=(
                pl.BlockSpec((16, part, width), lambda i, *_: (0, i, 0)),
                pl.BlockSpec((8, 2, part, BLK), lambda i, *_: (0, 0, i, 0)),
                pl.BlockSpec((2 * BLK, width), lambda i, *_: (0, 0)),
                pl.BlockSpec((2, 8, BLK), lambda i, *_: (0, 0, 0)),
            ),
            scratch_shapes=[pltpu.VMEM((orbs, part, width), bf16)],
        ),
        out_shape=(
            jax.ShapeDtypeStruct((16, depth, width), bf16),
            jax.ShapeDtypeStruct((8, 2, depth, BLK), bf16),
            jax.ShapeDtypeStruct((2 * BLK, width), f32),
            jax.ShapeDtypeStruct((2, 8, BLK), f32),
        ),
        compiler_params=pltpu.CompilerParams(vmem_limit_bytes=58 * 2**20),
    )(rows, order, valid, owner, energy_occ, b_slab, energy_vir.reshape(1, -1))
    cols = total // 8
    call = lambda one_way: pl.pallas_call(
        functools.partial(pairs, one_way),
        out_shape=(
            jax.ShapeDtypeStruct((width, cols), f32),
            jax.ShapeDtypeStruct((8, BLK), f32),
        ),
        in_specs=[vmem, pl.BlockSpec(memory_space=pl.ANY), vmem, vmem],
        out_specs=(vmem, vmem),
        scratch_shapes=[
            pltpu.VMEM((16, depth, width), bf16),
            dma(()),
            pltpu.VMEM((4, 2 * BLK + 16, width), jnp.int16),
            dma((4,)),
            dma((4,)),
            pltpu.VMEM((8, depth, BLK), bf16),
            pltpu.VMEM((8, depth, BLK), bf16),
            pltpu.VMEM((8, depth, BLK), bf16),
            pltpu.VMEM((8, 2, depth, BLK), bf16),
            pltpu.VMEM((4, 2, BLK + 16, width), jnp.int16),
            pltpu.VMEM((4, 2, BLK + 16, width), jnp.int16),
            pltpu.VMEM((4, 2, BLK, width), f32),
            pltpu.VMEM((4, 2 * BLK + 16, width), jnp.int16),
            pltpu.VMEM((4, 2 * BLK + 16, width), jnp.int16),
            pltpu.VMEM((8, 2 * BLK, width), bf16),
            pltpu.VMEM((8, 2 * BLK, cols), bf16),
            pltpu.VMEM((4, 8, BLK), f32),
            pltpu.VMEM((8, 8, BLK), f32),
            pltpu.VMEM((8, BLK), f32),
            dma((8,)), dma((8,)), dma((8,)), dma((8,)), dma((8,)), dma((8,)),
            dma((4, 2)), dma((4, 2)), dma((4,)), dma((4,)), dma((4,)),
            dma((8,)), dma((8,)), dma((8,)), dma((8,)),
            dma((8, 2)), dma((8,)),
            dma((3,)), dma((3,)), dma((7,)), dma((7,)),
        ],
        compiler_params=pltpu.CompilerParams(
            collective_id=1 if one_way else 2, has_side_effects=True, vmem_limit_bytes=48 * 2**20
        ),
    )
    density, occupied = lax.cond(one_way, call(True), call(False), cut, left, coef, hits)
    return density, occupied[0, : owner.shape[0]]


def solution(mesh):
    fits = mesh.shape["aux"] == 8 and mesh.shape["rep"] == 4
    return jax.shard_map(
        local if fits else plain,
        mesh=mesh,
        in_specs=(P("aux", None, "rep"), P(), P(), P(), P("aux", None, None), P("aux")),
        out_specs=(P("rep", "aux"), P()),
        check_vma=False,
    )
```

```python
import functools

import jax
import jax.numpy as jnp
from jax import lax
from jax.experimental import pallas as pl
from jax.experimental.pallas import tpu as pltpu
from jax.sharding import PartitionSpec as P

BLK = 128


def plain(b_slab, energy_occ, energy_vir, owner, tasks, counts):
    aux_count = lax.axis_size("aux")
    rep_count = lax.axis_size("rep")
    width = b_slab.shape[2]
    slots = tasks.shape[1]
    occ_total = owner.shape[0]
    occ_local = occ_total // aux_count
    total = energy_vir.shape[0]
    rep_rank = lax.axis_index("rep")
    aux_rank = lax.axis_index("aux")
    rows = jnp.concatenate([tasks.reshape(1, -1), counts.reshape(1, 1)], axis=1)
    rows = lax.all_gather(rows, "aux", axis=0, tiled=True)
    all_tasks = rows[:, :-1].reshape(aux_count, slots, 3)
    base = jnp.arange(aux_count, dtype=jnp.int32)[:, None] * occ_local
    first = owner[base + all_tasks[:, :, 0]].reshape(-1)
    second = owner[base + all_tasks[:, :, 1]].reshape(-1)
    start = all_tasks[:, :, 2].reshape(-1) * BLK
    holder = start // width
    within = start - holder * width
    number = first.shape[0]

    blocks = []
    for t in range(number):
        piece = lax.dynamic_slice(b_slab, (0, second[t], within[t]), (b_slab.shape[0], 1, BLK))[:, 0, :]
        blocks.append(jnp.where(holder[t] == rep_rank, piece, jnp.zeros_like(piece)))
    right = lax.psum(jnp.stack(blocks), "rep")
    left = jnp.take(b_slab, first, axis=1)
    part = jnp.einsum("tpc,pta->tca", right, left, preferred_element_type=jnp.float32)
    coulomb = lax.psum_scatter(part, "aux", scatter_dimension=0, tiled=True)

    mine = lambda v: lax.dynamic_slice_in_dim(v, aux_rank * slots, slots)
    my_first, my_second, my_start = mine(first), mine(second), mine(start)
    quarter = lax.dynamic_slice_in_dim(energy_vir, rep_rank * width, width)
    pair = energy_occ[my_first] + energy_occ[my_second]
    block_energy = jnp.stack([lax.dynamic_slice_in_dim(energy_vir, my_start[t], BLK) for t in range(slots)])
    denominator = pair[:, None, None] - block_energy[:, :, None] - quarter[None, None, :]
    live = jnp.arange(slots, dtype=jnp.int32) < counts[0]
    amplitude = jnp.where(live[:, None, None], coulomb / denominator, jnp.zeros_like(coulomb))
    weight = jnp.sum(amplitude * amplitude, axis=(1, 2))
    orbs = jnp.arange(occ_total, dtype=jnp.int32)
    hits = (my_first[:, None] == orbs).astype(jnp.float32) + (my_second[:, None] == orbs).astype(jnp.float32)
    occupied = lax.psum(-jnp.sum(weight[:, None] * hits, axis=0), ("aux", "rep"))

    amp = amplitude.astype(jnp.bfloat16).reshape(slots * BLK, width)
    amps = lax.all_gather(amp, "aux", axis=0, tiled=True)
    cols = total // aux_count
    where = aux_rank * cols
    own = lax.dynamic_slice_in_dim(amps, lax.rem(where, width), cols, 1)
    own = jnp.where(where // width == rep_rank, own, jnp.zeros_like(own))
    own = lax.psum(own, "rep")
    density = lax.dot_general(amps, own, (((0,), (0,)), ((), ())), preferred_element_type=jnp.float32)
    return density, occupied


MESH = pl.DeviceIdType.MESH


def greet(peers):
    barrier = pltpu.get_barrier_semaphore()
    for peer in peers:
        pl.semaphore_signal(barrier, inc=1, device_id=peer, device_id_type=MESH)
    pl.semaphore_wait(barrier, len(peers))


def send(src, dst, send_sem, recv_sem, peer):
    return pltpu.make_async_remote_copy(
        src_ref=src, dst_ref=dst, send_sem=send_sem, recv_sem=recv_sem, device_id=peer, device_id_type=MESH
    )


def spread_rows(row_ref, rows_ref, mine, landed, rows_send, rows_recv):
    p = lax.axis_index("aux")
    r = lax.axis_index("rep")
    peers = [(lax.rem(p + 1 + s, 8), r) for s in range(7)]
    greet(peers)
    mine[...] = row_ref[...]
    landed[p] = row_ref[...]
    copies = [send(mine, landed.at[p], rows_send.at[s], rows_recv.at[s], peers[s]) for s in range(7)]
    for copy in copies:
        copy.start()
    for copy in copies:
        copy.wait()
    rows_ref[...] = landed[...]


def select(rows, order, valid, owner, e_occ, b_ref, e_row, left, cut, coef, hits, wide):
    p = lax.axis_index("aux")
    r = lax.axis_index("rep")
    depth, orbs, width = b_ref.shape

    def field(k, s, which):
        task = order[2 * k + s]
        return rows[task // 2, 0, 3 * lax.rem(task, 2) + which]

    def orbital(k, s, which):
        return owner[order[2 * k + s] // 2 * 2 + field(k, s, which)]

    wide[...] = jnp.swapaxes(b_ref[...], 0, 1)
    for k in range(8):
        for s in range(2):
            i, j = orbital(k, s, 0), orbital(k, s, 1)
            left[2 * k + s] = wide[i]
            start = field(k, s, 2) * BLK
            holder = start // width
            within = pl.multiple_of(start - holder * width, BLK)
            mask = jnp.full((1, BLK), jnp.where(holder == r, 1.0, 0.0), jnp.float32).astype(jnp.bfloat16)
            cut[k, s] = wide[j, :, pl.ds(within, BLK)] * mask

    @pl.when(pl.program_id(0) == 0)
    def _():
        lanes = lax.broadcasted_iota(jnp.int32, (8, BLK), 1)
        quarter = e_row[:, pl.ds(pl.multiple_of(r * width, BLK), width)]
        for s in range(2):
            i, j = orbital(p, s, 0), orbital(p, s, 1)
            start = pl.multiple_of(field(p, s, 2) * BLK, BLK)
            live = jnp.where(valid[2 * p + s] > 0, 1.0, 0.0)
            column = jnp.broadcast_to(e_row[:, pl.ds(start, BLK)], (BLK, BLK)).T[:, :1]
            denominator = (e_occ[i] + e_occ[j]) - column - quarter
            coef[s * BLK:(s + 1) * BLK, :] = live / denominator
            hits[s] = (lanes == i).astype(jnp.float32) + (lanes == j).astype(jnp.float32)


def pack(dst, x):
    rows = x.shape[0]
    top = jnp.max(jnp.abs(x), axis=0, keepdims=True)
    power = jnp.ceil(jnp.log2(jnp.maximum(top, 1e-30)))
    scaled = jnp.floor(x * jnp.exp2(14.0 - power) + 0.5)
    dst[:rows, :] = scaled.astype(jnp.int32).astype(jnp.int16)
    dst[rows:, :] = jnp.broadcast_to(power, (16, x.shape[1])).astype(jnp.int32).astype(jnp.int16)


def unpack(src):
    rows = src.shape[0] - 16
    power = src[rows:, :].astype(jnp.int32).astype(jnp.float32)[:1]
    return src[:rows, :].astype(jnp.int32).astype(jnp.float32) * jnp.exp2(power - 14.0)


def pairs(one_way, cut, left_hbm, coef, hits, dens, occ,
          left, left_sem, z_out, e_s, e_r, cut_in, chip, chip_in, block, y_out, y_in, acc, up_in, down_in, amps, own, occ_rep, occ_aux, occ_sum,
          a_s, a_r, b_s, b_r, c_s, c_r, y_s, y_r, z_s, u_r, d_r, gu_s, gd_s, gy_s, g_r, h_s, h_r, or_s, or_r, oa_s, oa_r):
    p = lax.axis_index("aux")
    r = lax.axis_index("rep")
    z, y = p // 2, lax.rem(p, 2)
    core = lax.rem(r, 2)
    twin = (p, r + 1 - 2 * core)
    across = (p, lax.rem(r + 2, 4))
    y_peer = (p + 1 - 2 * y, r)
    above = (lax.rem(p + 2, 8), r)
    below = (lax.rem(p + 6, 8), r)
    reps = [(p, lax.rem(r + 1 + s, 4)) for s in range(3)]
    auxes = [(lax.rem(p + 1 + s, 8), r) for s in range(7)]
    width = left.shape[2]
    cols = own.shape[2]
    fetch = pltpu.make_async_copy(left_hbm, left, left_sem)
    fetch.start()
    greet(reps + auxes)

    def place(m):
        first = jnp.where(m == 0, 3, jnp.where(m == 1, 0, jnp.where(m == 2, 2, 1)))
        return first + (z // 2) * (3 - 2 * first)

    def copy_a(k):
        return send(cut.at[k, 1 - core], cut_in.at[k], a_s.at[k], a_r.at[k], twin)

    def copy_b(k):
        return send(chip.at[k], chip_in.at[k], b_s.at[k], b_r.at[k], across)

    def copy_c(k, half):
        return send(block.at[k, half], block.at[k, half], c_s.at[k], c_r.at[k], twin)

    x = r // 2

    def slot_a(t):
        return send(cut.at[2 * t + 1 - core, x], cut_in.at[t], a_s.at[t], a_r.at[t], twin)

    def slot_b(t, side):
        return send(block.at[2 * t + core, side], block.at[2 * t + core, side], b_s.at[t], b_r.at[t], across)

    def slot_c(t, side):
        return send(block.at[2 * t + core, side], block.at[2 * t + core, side], c_s.at[t], c_r.at[t], twin)

    def slot_e(t, side):
        return send(block.at[2 * t + core, side], block.at[2 * t + core, side], e_s.at[t], e_r.at[t], twin)

    def slots_a(m, carry):
        slot_a(place(m)).start()
        return carry

    def slots_b(m, carry):
        t = place(m)
        slot_a(t).wait_recv()
        block[2 * t + core, x] = cut[2 * t + core, x] + cut_in[t]
        slot_b(t, x).start()
        slot_e(t, x).start()
        return carry

    def phase_a(m, carry):
        for u in range(2):
            k = 2 * place(m) + u
            copy_a(k).start()
        return carry

    def phase_b(m, carry):
        for u in range(2):
            k = 2 * place(m) + u
            copy_a(k).wait_recv()
            chip[k] = cut[k, core] + cut_in[k]
            copy_b(k).start()
        return carry

    lax.fori_loop(0, 4, slots_a if one_way else phase_a, 0)
    lax.fori_loop(0, 4, slots_b if one_way else phase_b, 0)
    fetch.wait()

    def copy_y(t, s):
        return send(y_out.at[t, s], y_in.at[t, s], y_s.at[t, s], y_r.at[t, s], y_peer)

    def copy_up(t):
        return send(z_out.at[t], up_in.at[t], z_s.at[t], u_r.at[t], above)

    def copy_down(t):
        return send(z_out.at[t], down_in.at[t], z_s.at[t], d_r.at[t], below)

    def gather_sum(t):
        for s in range(2):
            copy_y(t, s).wait_recv()
            acc[t, s] = acc[t, s] + unpack(y_in.at[t, s])

        @pl.when((z <= t) & (z > 0))
        def _():
            copy_up(t).wait_recv()
            acc[t] = acc[t] + unpack(up_in.at[t]).reshape(2, BLK, width)

        @pl.when((z >= t) & (z < 3))
        def _():
            copy_down(t).wait_recv()
            acc[t] = acc[t] + unpack(down_in.at[t]).reshape(2, BLK, width)

    def pass_on(t):
        @pl.when(t != z)
        def _():
            gather_sum(t)
            pack(z_out.at[t], acc[t].reshape(2 * BLK, width))

        @pl.when(t > z)
        def _():
            copy_up(t).start()

        @pl.when(t < z)
        def _():
            copy_down(t).start()

    def product(k, s):
        return lax.dot_general(
            block[k, s], left[2 * k + s], (((0,), (0,)), ((), ())), preferred_element_type=jnp.float32
        )

    def partial(t, s):
        pack(y_out.at[t, s], product(2 * t + 1 - y, s))
        copy_y(t, s).start()
        acc[t, s] = product(2 * t + y, s)

    def near(m, carry):
        t = place(m)
        slot_e(t, x).wait_recv()
        partial(t, x)
        return carry

    if one_way:
        lax.fori_loop(0, 4, near, 0)

    inner = (z > 0) & (z < 3)
    lag = jnp.where(inner, 2, 1)

    def phase_c(m, carry):
        t = place(m)
        if one_way:
            slot_b(t, 1 - x).wait_recv()
            slot_c(t, 1 - x).start()
            slot_c(t, 1 - x).wait_recv()
            partial(t, 1 - x)
        else:
            for u in range(2):
                k = 2 * t + u
                copy_b(k).wait_recv()
                block[k, core] = chip[k] + chip_in[k]
                copy_c(k, core).start()
            for u in range(2):
                copy_c(2 * t + u, 1 - core).wait_recv()
            for s in range(2):
                partial(t, s)

        @pl.when(m >= lag)
        def _():
            pass_on(place(m - lag))

        return carry

    lax.fori_loop(0, 4, phase_c, 0)

    @pl.when(inner)
    def _():
        pass_on(place(2))

    pass_on(place(3))
    gather_sum(z)

    found = jnp.zeros((8, BLK), jnp.float32)
    for s in range(2):
        amplitude = acc[z, s] * coef[s * BLK:(s + 1) * BLK, :]
        square = jnp.sum(amplitude * amplitude, axis=0, keepdims=True)
        weight = jnp.sum(square, axis=1, keepdims=True)
        found = found - weight * hits[s]
        amps[p, s * BLK:(s + 1) * BLK, :] = amplitude.astype(jnp.bfloat16)
    occ_rep[r] = found

    def copy_or(s):
        return send(occ_rep.at[r], occ_rep.at[r], or_s.at[s], or_r.at[s], reps[s])

    def copy_oa(s):
        return send(occ_sum, occ_aux.at[p], oa_s.at[s], oa_r.at[s], auxes[s])

    holder = (p * cols) // width
    offset = pl.multiple_of(p * cols - holder * width, BLK)

    def copy_gu(k):
        return send(amps.at[k], amps.at[k], gu_s.at[k], g_r.at[k], above)

    def copy_gd(k):
        return send(amps.at[k], amps.at[k], gd_s.at[k], g_r.at[k], below)

    def copy_gy(k):
        return send(amps.at[k], amps.at[k], gy_s.at[k], g_r.at[k], y_peer)

    relay = r == lax.rem(holder + 2, 4)

    def copy_h(k, s):
        return send(amps.at[k, :, pl.ds(offset, cols)], own.at[k], h_s.at[k, s], h_r.at[k], (twin, across)[s])

    def copy_relay(k):
        return send(own.at[k], own.at[k], h_s.at[k, 0], h_r.at[k], twin)

    def share(k):
        @pl.when(r == holder)
        def _():
            copy_h(k, 1).start()
            copy_h(k, 0).start()
            own[k] = amps[k, :, pl.ds(offset, cols)]

    def when_up(k, d, act):
        @pl.when((z < 3) & (d <= 0))
        def _():
            act(copy_gu(k))

    def when_down(k, d, act):
        @pl.when((z > 0) & (d >= 0))
        def _():
            act(copy_gd(k))

    def at(act_fn, *offsets):
        for d in offsets:
            t = z + d

            @pl.when((t >= 0) & (t < 4))
            def _():
                act_fn(t, d)

    def gather(t, d):
        k = 2 * t + y
        if d != 0:
            copy_gy(k).wait_recv()
        when_up(k, d, lambda c: c.start())
        when_down(k, d, lambda c: c.start())
        copy_gy(k).start()
        share(k)

    def gather_y(t, d):
        k = 2 * t + 1 - y
        copy_gy(k).wait_recv()
        share(k)

    def multiply(t, d):
        @pl.when(r != holder)
        def _():
            for u in range(2):
                copy_h(2 * t + u, 0).wait_recv()

                @pl.when(relay)
                def _():
                    copy_relay(2 * t + u).start()

        more = lax.dot_general(
            amps[pl.ds(2 * t, 2)].reshape(4 * BLK, width), own[pl.ds(2 * t, 2)].reshape(4 * BLK, cols),
            (((0,), (0,)), ((), ())), preferred_element_type=jnp.float32,
        )
        dens[...] = more if d == 0 else dens[...] + more

    at(gather, 0)
    for s in range(3):
        copy_or(s).start()
    at(gather, 1, -1)
    at(gather_y, 0)
    for s in range(3):
        copy_or(s).wait_recv()
    occ_sum[...] = occ_rep[0] + occ_rep[1] + occ_rep[2] + occ_rep[3]
    occ_aux[p] = occ_sum[...]
    for s in range(7):
        copy_oa(s).start()
    at(gather, 2, -2)
    at(gather_y, 1)
    at(multiply, 0)
    at(gather, 3, -3)
    at(gather_y, -1)
    at(multiply, 1)
    at(gather_y, 2)
    at(multiply, -1)
    at(gather_y, -2)
    at(multiply, 2)
    at(gather_y, 3)
    at(multiply, -2)
    at(gather_y, -3)
    at(multiply, 3, -3)
    for s in range(7):
        copy_oa(s).wait_recv()
    total = occ_aux[0]
    for k in range(1, 8):
        total = total + occ_aux[k]
    occ[...] = total

    if not one_way:
        for k in range(8):
            copy_a(k).wait_send()
            copy_b(k).wait_send()
            copy_c(k, core).wait_send()
    for t in range(4):
        if one_way:
            slot_a(t).wait_send()
            slot_b(t, x).wait_send()
            slot_c(t, x).wait_send()
            slot_e(t, x).wait_send()
        for s in range(2):
            copy_y(t, s).wait_send()

        @pl.when(t != z)
        def _():
            copy_up(t).wait_send()

    def sent(t, d):
        k = 2 * t + y
        when_up(k, d, lambda c: c.wait_send())
        when_down(k, d, lambda c: c.wait_send())
        copy_gy(k).wait_send()

    at(sent, 0, 1, -1, 2, -2, 3, -3)

    @pl.when(r == holder)
    def _():
        for k in range(8):
            for s in range(2):
                copy_h(k, s).wait_send()

    @pl.when(relay)
    def _():
        for k in range(8):
            copy_relay(k).wait_send()

    for s in range(3):
        copy_or(s).wait_send()
    for s in range(7):
        copy_oa(s).wait_send()


def local(b_slab, energy_occ, energy_vir, owner, tasks, counts):
    depth, orbs, width = b_slab.shape
    total = energy_vir.shape[0]
    row = jnp.concatenate([tasks.reshape(-1), counts.reshape(-1)])
    row = jnp.broadcast_to(jnp.pad(row, (0, BLK - row.shape[0]))[None], (8, BLK))
    part = 192
    dma = pltpu.SemaphoreType.DMA
    vmem = pl.BlockSpec(memory_space=pltpu.VMEM)
    f32, bf16 = jnp.float32, jnp.bfloat16
    rows = pl.pallas_call(
        spread_rows,
        out_shape=jax.ShapeDtypeStruct((8, 8, BLK), jnp.int32),
        in_specs=[vmem],
        out_specs=vmem,
        scratch_shapes=[
            pltpu.VMEM((8, BLK), jnp.int32), pltpu.VMEM((8, 8, BLK), jnp.int32), dma((7,)), dma((7,)),
        ],
        compiler_params=pltpu.CompilerParams(collective_id=0, has_side_effects=True),
    )(row)
    counts_all = rows[:, 0, 6]
    number = 2 * counts_all.shape[0]
    ids = jnp.arange(number, dtype=jnp.int32)
    side = (rows[:, 0, 2:6:3].reshape(-1) * BLK >= total // 2).astype(jnp.int32)
    alive = (jnp.arange(2, dtype=jnp.int32)[None, :] < counts_all[:, None]).reshape(-1)
    ahead = (ids[:, None] > ids[None, :]) & (side[:, None] == side[None, :]) & alive[None, :]
    rank = jnp.sum(ahead.astype(jnp.int32), axis=1)
    seat = jnp.where(alive, 2 * rank + side, 2 * number)
    one_way = jnp.max(seat * alive) < number
    taken = seat[None, :] == ids[:, None]
    order = jnp.where(one_way, jnp.sum(taken * ids[None, :], axis=1), ids)
    valid = jnp.where(one_way, jnp.sum(taken.astype(jnp.int32), axis=1), alive.astype(jnp.int32))
    left, cut, coef, hits = pl.pallas_call(
        select,
        grid_spec=pltpu.PrefetchScalarGridSpec(
            num_scalar_prefetch=5,
            grid=(depth // part,),
            in_specs=[
                pl.BlockSpec((part, orbs, width), lambda i, *_: (i, 0, 0)),
                pl.BlockSpec((1, total), lambda i, *_: (0, 0)),
            ],
            out_specs=(
                pl.BlockSpec((16, part, width), lambda i, *_: (0, i, 0)),
                pl.BlockSpec((8, 2, part, BLK), lambda i, *_: (0, 0, i, 0)),
                pl.BlockSpec((2 * BLK, width), lambda i, *_: (0, 0)),
                pl.BlockSpec((2, 8, BLK), lambda i, *_: (0, 0, 0)),
            ),
            scratch_shapes=[pltpu.VMEM((orbs, part, width), bf16)],
        ),
        out_shape=(
            jax.ShapeDtypeStruct((16, depth, width), bf16),
            jax.ShapeDtypeStruct((8, 2, depth, BLK), bf16),
            jax.ShapeDtypeStruct((2 * BLK, width), f32),
            jax.ShapeDtypeStruct((2, 8, BLK), f32),
        ),
        compiler_params=pltpu.CompilerParams(vmem_limit_bytes=58 * 2**20),
    )(rows, order, valid, owner, energy_occ, b_slab, energy_vir.reshape(1, -1))
    cols = total // 8
    call = lambda one_way: pl.pallas_call(
        functools.partial(pairs, one_way),
        out_shape=(
            jax.ShapeDtypeStruct((width, cols), f32),
            jax.ShapeDtypeStruct((8, BLK), f32),
        ),
        in_specs=[vmem, pl.BlockSpec(memory_space=pl.ANY), vmem, vmem],
        out_specs=(vmem, vmem),
        scratch_shapes=[
            pltpu.VMEM((16, depth, width), bf16),
            dma(()),
            pltpu.VMEM((4, 2 * BLK + 16, width), jnp.int16),
            dma((4,)),
            dma((4,)),
            pltpu.VMEM((8, depth, BLK), bf16),
            pltpu.VMEM((8, depth, BLK), bf16),
            pltpu.VMEM((8, depth, BLK), bf16),
            pltpu.VMEM((8, 2, depth, BLK), bf16),
            pltpu.VMEM((4, 2, BLK + 16, width), jnp.int16),
            pltpu.VMEM((4, 2, BLK + 16, width), jnp.int16),
            pltpu.VMEM((4, 2, BLK, width), f32),
            pltpu.VMEM((4, 2 * BLK + 16, width), jnp.int16),
            pltpu.VMEM((4, 2 * BLK + 16, width), jnp.int16),
            pltpu.VMEM((8, 2 * BLK, width), bf16),
            pltpu.VMEM((8, 2 * BLK, cols), bf16),
            pltpu.VMEM((4, 8, BLK), f32),
            pltpu.VMEM((8, 8, BLK), f32),
            pltpu.VMEM((8, BLK), f32),
            dma((8,)), dma((8,)), dma((8,)), dma((8,)), dma((8,)), dma((8,)),
            dma((4, 2)), dma((4, 2)), dma((4,)), dma((4,)), dma((4,)),
            dma((8,)), dma((8,)), dma((8,)), dma((8,)),
            dma((8, 2)), dma((8,)),
            dma((3,)), dma((3,)), dma((7,)), dma((7,)),
        ],
        compiler_params=pltpu.CompilerParams(
            collective_id=1 if one_way else 2, has_side_effects=True, vmem_limit_bytes=48 * 2**20
        ),
    )
    density, occupied = lax.cond(one_way, call(True), call(False), cut, left, coef, hits)
    return density, occupied[0, : owner.shape[0]]


def solution(mesh):
    fits = mesh.shape["aux"] == 8 and mesh.shape["rep"] == 4
    return jax.shard_map(
        local if fits else plain,
        mesh=mesh,
        in_specs=(P("aux", None, "rep"), P(), P(), P(), P("aux", None, None), P("aux")),
        out_specs=(P("rep", "aux"), P()),
        check_vma=False,
    )
```
